32 devices in a mesh: section: 8 (over z, core), seq: 4 (over y, x).
Axes of the slice: x: 2, y: 2, z: 4, core: 2. Of those that a mesh axis runs over, the one named last changes fastest.
Arguments:
- layer_input: bfloat16 [8, 3, 4096, 768], P('section', None, 'seq'), may hold values from -6 to 6
- grad_out: bfloat16 [8, 3, 4096, 768], P('section', None, 'seq'), may hold values from -6 to 6
- gate_weight: bfloat16 [768, 768], P('seq'), may hold values from -0.21875 to 0.21875
- mix_in_right: bfloat16 [64, 64, 64], P('seq'), may hold values from -0.75 to 0.75
- mix_in_left: bfloat16 [64, 64, 64], P('seq'), may hold values from -0.75 to 0.75
- mix_out_left: bfloat16 [64, 64, 64], P('seq'), may hold values from -0.75 to 0.75
- mix_out_right: bfloat16 [64, 64, 64], P('seq'), may hold values from -0.75 to 0.75
- kernel: bfloat16 [4096, 768], P('seq'), may hold values from -5 to 5
Outputs:
- input_grad: bfloat16 [8, 3, 4096, 768], P('section', None, 'seq')
- weight_grad: float32 [768, 768], P('seq')
- kernel_grad: bfloat16 [4096, 768], P('seq')
The draws below stay inside these ranges and needn't reach their ends.
All inputs are finite; a program needn't handle non-finite values.
Results may differ from the reference program's by a relative error of at most 0.007.
Values may be sent and summed in bfloat16 or wider, within the bound.
No kernel may reach another device: no remote copies, remote signals or barrier semaphores. Data moves between devices by JAX's collectives and lax.ppermute only.
A program may use at most 128 MiB of HBM per device.

```python
import math
import jax
import jax.numpy as jnp
from jax import lax

D = 768
BLOCK = 64
BATCH = 3
SEQ = 4096
REPLICAS = 8


def raised(drawn, key, source, target, shards_of, factor):
    def block_of(position):
        return (jnp.arange(drawn.shape[position]) // (drawn.shape[position] // shards_of)).reshape((-1,) + (1,) * (drawn.ndim - 1 - position))

    one_side = jax.random.permutation(key, shards_of)[block_of(target)]
    other_side = (block_of(target) + shards_of // 2) % shards_of
    return jnp.where((block_of(source) == one_side) | (block_of(source) == other_side), factor * drawn, drawn)


def levels(rng, shape, shards, least, top_value):
    level = 1.0
    for position, shards_of in shards:
        draws = jax.random.uniform(jax.random.fold_in(jax.random.fold_in(rng, 6), position), (shards_of,), jnp.float32, least / len(shards), top_value / len(shards))
        level = level * jnp.repeat(jnp.exp(draws), shape[position] // shards_of).reshape((-1,) + (1,) * (len(shape) - 1 - position))
    return level


def gaussian(rng, extent, width, reach, split=(), held_as=jnp.bfloat16):
    values = width * jax.random.normal(rng, extent, jnp.float32)
    if split:
        values = values * levels(rng, extent, split, -0.22, 0.18)
    return jnp.clip(values, -reach, reach).astype(held_as)


def noise_with(own_key, dims, width, reach, cuts, heavy, kind=jnp.bfloat16):
    values = width * jax.random.normal(own_key, dims, jnp.float32)
    if cuts:
        values = values * levels(own_key, dims, cuts, -0.22, 0.18)
    return jnp.clip(raised(values, jax.random.fold_in(own_key, 3), *heavy), -reach, reach).astype(kind)


def setup_inputs(seed: int = 0) -> dict:
    key_list = jax.random.split(jax.random.key(seed), 9)
    return {
        "layer_input": noise_with(key_list[0], (REPLICAS, BATCH, SEQ, D), 1.0, 6.0, ((0, 8), (2, 4)), (2, 3, 4, 2.0)),
        "grad_out": gaussian(key_list[1], (REPLICAS, BATCH, SEQ, D), 1.0, 6.0, ((0, 8), (2, 4))),
        "gate_weight": gaussian(key_list[2], (D, D), D ** -0.5, 0.21875, ((0, 4),)),
        "mix_in_right": gaussian(key_list[3], (BLOCK, BLOCK, BLOCK), BLOCK ** -0.5, 0.75, ((0, 4),)),
        "mix_in_left": gaussian(key_list[4], (BLOCK, BLOCK, BLOCK), BLOCK ** -0.5, 0.75, ((0, 4),)),
        "mix_out_left": gaussian(key_list[5], (BLOCK, BLOCK, BLOCK), BLOCK ** -0.5, 0.75, ((0, 4),)),
        "mix_out_right": gaussian(key_list[6], (BLOCK, BLOCK, BLOCK), BLOCK ** -0.5, 0.75, ((0, 4),)),
        "kernel": gaussian(key_list[7], (SEQ, D), 1.0, 5.0, ((0, 4),)),
    }


def mix_product(form, left, right):
    return jnp.einsum(form, left.astype(jnp.float32), right.astype(jnp.float32))

def one_replica(inputs, gate_weight, right_in, left_in, left_out, right_out, kernel):
    layer_input, grad_out = inputs
    count_batch = layer_input.shape[0]
    acts = layer_input.reshape(count_batch, BLOCK, BLOCK, D)
    kern = kernel.reshape(BLOCK, BLOCK, D).astype(jnp.float32)
    first_mixed = mix_product('aic,bacd->baid', right_in, acts).astype(jnp.bfloat16)
    second_mixed = mix_product('ija,baid->bijd', left_in, first_mixed)
    weighted = (second_mixed * kern).astype(jnp.bfloat16)
    third_mixed = mix_product('ikj,bijd->bikd', left_out, weighted).astype(jnp.bfloat16)
    mixed = mix_product('kmi,bikd->bkmd', right_out, third_mixed).reshape(count_batch * SEQ, D)
    flat_input = layer_input.reshape(count_batch * SEQ, D)
    upstream = grad_out.reshape(count_batch * SEQ, D).astype(jnp.float32)
    preact = jnp.dot(flat_input, gate_weight, preferred_element_type=jnp.float32)
    sigma = jax.nn.sigmoid(preact)
    swish = preact * sigma
    slope = sigma * (1.0 + preact * (1.0 - sigma))
    mix_grad = (upstream * swish).astype(jnp.bfloat16).reshape(count_batch, BLOCK, BLOCK, D)
    gate_grad = (upstream * mixed * slope).astype(jnp.bfloat16)
    weight_sum = jnp.dot(flat_input.T, gate_grad, preferred_element_type=jnp.float32)
    gate_part = jnp.dot(gate_grad, gate_weight.T, preferred_element_type=jnp.float32)
    back_third = mix_product('kmi,bkmd->bkid', right_out, mix_grad).astype(jnp.bfloat16)
    back_second = mix_product('ikj,bkid->bijd', left_out, back_third)
    kernel_sum = lax.optimization_barrier(jnp.sum(second_mixed * back_second, axis=0)).reshape(SEQ, D)
    back_weighted = (back_second * kern).astype(jnp.bfloat16)
    back_first = mix_product('ija,bijd->biad', left_in, back_weighted).astype(jnp.bfloat16)
    mix_part = mix_product('aic,biad->bacd', right_in, back_first).reshape(count_batch * SEQ, D)
    input_grad = (gate_part + mix_part).astype(jnp.bfloat16).reshape(count_batch, SEQ, D)
    return (input_grad, weight_sum, kernel_sum)

def reference(layer_input, grad_out, gate_weight, mix_in_right, mix_in_left, mix_out_left, mix_out_right, kernel):

    def run_one(inputs):
        return one_replica(inputs, gate_weight, mix_in_right, mix_in_left, mix_out_left, mix_out_right, kernel)
    input_grad, weight_sums, kernel_sums = lax.map(run_one, (layer_input, grad_out))
    weight_grad = lax.optimization_barrier(jnp.sum(weight_sums, axis=0)) * (1.0 / math.sqrt(REPLICAS * BATCH * SEQ))
    kernel_grad = (lax.optimization_barrier(jnp.sum(kernel_sums, axis=0)) * (1.0 / math.sqrt(REPLICAS * BATCH))).astype(jnp.bfloat16)
    return (input_grad, weight_grad, kernel_grad)
```

```python
import functools
import math

import jax
import jax.numpy as jnp
from jax import lax
from jax.experimental import pallas as pl
from jax.experimental.pallas import tpu as pltpu
from jax.sharding import PartitionSpec as P

BATCH = 3
SEQ = 4096
HALF = 8

BF16 = jnp.bfloat16
F32 = jnp.float32


def contract(form, left, right):
    return jnp.einsum(form, left, right, preferred_element_type=jnp.float32)


def dot(left, right):
    return jnp.dot(left, right, preferred_element_type=F32)


def dot_first(left, right):
    return lax.dot_general(left, right, (((0,), (0,)), ((), ())), preferred_element_type=F32)


def dot_last(left, right):
    return lax.dot_general(left, right, (((1,), (1,)), ((), ())), preferred_element_type=F32)


def params(grid):
    return pltpu.CompilerParams(
        dimension_semantics=("arbitrary",) * len(grid), vmem_limit_bytes=56 * 1024 * 1024
    )


def cost(flops, bytes_accessed):
    return pl.CostEstimate(flops=int(flops), bytes_accessed=int(bytes_accessed), transcendentals=0)


def put_pair(outs, where, low, first, second, own):
    for r, out in enumerate(outs):
        for g in range(own // HALF):
            at = r * own + g * HALF
            rows = jnp.concatenate([first[at : at + HALF], second[at : at + HALF]], axis=0)
            out[where, g, low : low + 2 * HALF, :] = rows.astype(BF16)


def expand_kernel(devices, left_in, left_out, right_in, right_out, *outs):
    big_li, big_qo, big_pt, big_rt, small_qt, small_lt = outs
    own, block = left_in.shape[0], left_in.shape[1]
    wide = block * HALF
    s = lax.broadcasted_iota(jnp.int32, (block, wide), 0)
    lane = lax.broadcasted_iota(jnp.int32, (block, wide), 1)
    picks = [
        jnp.where(lane == s * HALF + t, 1.0, 0.0).astype(BF16) for t in range(HALF)
    ]
    row = lax.broadcasted_iota(jnp.int32, (block, block), 0)
    column = lax.broadcasted_iota(jnp.int32, (block, block), 1)
    same = jnp.where(row == column, 1.0, 0.0).astype(BF16)
    for p in range(own):
        g, t = divmod(p, HALF)
        rows = slice(t * block, (t + 1) * block)
        big_li[g, rows, :] = dot(left_in[p], picks[t]).astype(BF16)
        big_qo[g, rows, :] = dot(right_out[p], picks[t]).astype(BF16)
        big_pt[g, rows, :] = dot_first(left_out[p], picks[t]).astype(BF16)
        big_rt[g, rows, :] = dot_first(right_in[p], picks[t]).astype(BF16)
        small_qt[p] = dot_last(same, right_out[p]).astype(BF16)
        small_lt[p] = dot_last(same, left_in[p]).astype(BF16)


def expand(devices, left_in, left_out, right_in, right_out):
    own, block = left_in.shape[0], left_in.shape[1]
    big = jax.ShapeDtypeStruct((own // HALF, HALF * block, HALF * block), BF16)
    small = jax.ShapeDtypeStruct(left_in.shape, BF16)
    return pl.pallas_call(
        functools.partial(expand_kernel, devices),
        out_shape=(big,) * 4 + (small,) * 2,
        compiler_params=params(()),
        cost_estimate=cost(4e9, 8e6),
    )(left_in, left_out, right_in, right_out)


def first_kernel(devices, right_in, acts, *outs):
    own = right_in.shape[0]
    for p in range(0, own, 2):
        put_pair(
            outs, 0, p * HALF, dot(right_in[p], acts[0, p]), dot(right_in[p + 1], acts[0, p + 1]), own
        )


def first(devices, c, width, right_in, acts):
    batch, own, block, _ = acts.shape
    piece = jax.ShapeDtypeStruct((batch, own // HALF, own * HALF, width), BF16)
    grid = (batch,)
    return pl.pallas_call(
        functools.partial(first_kernel, devices),
        grid=grid,
        in_specs=[
            pl.BlockSpec(right_in.shape, lambda b: (0, 0, 0)),
            pl.BlockSpec((1, own, block, width), lambda b: (b, 0, 0, c)),
        ],
        out_specs=[pl.BlockSpec((1,) + piece.shape[1:], lambda b: (b, 0, 0, 0))] * devices,
        out_shape=(piece,) * devices,
        compiler_params=params(grid),
        cost_estimate=cost(2 * batch * own * block * block * width, 4 * batch * own * block * width),
    )(right_in, acts)


def middle_kernel(devices, small, big, kern, *refs):
    pieces, outs, second = refs[:devices], refs[devices:-1], refs[-1]
    half, block = small.shape[0], small.shape[1]
    own = block // devices
    scale = kern[0].astype(F32)
    for b in range(second.shape[0]):
        spread = jnp.concatenate([piece[b, 0] for piece in pieces], axis=0)
        value = dot(big[0], spread)
        second[b, 0] = value
        weighted = (value * scale).astype(BF16)
        for i in range(0, half, 2):
            low = dot(small[i], weighted[i * block : (i + 1) * block])
            high = dot(small[i + 1], weighted[(i + 1) * block : (i + 2) * block])
            put_pair(outs, b, i * HALF, low, high, own)


def middle(devices, c, width, small, big, kern, pieces):
    batch, parts, long, _ = pieces[0].shape
    block = small.shape[1]
    piece = jax.ShapeDtypeStruct(pieces[0].shape, BF16)
    second = jax.ShapeDtypeStruct((batch, parts, HALF * block, width), F32)
    grid = (parts,)
    return pl.pallas_call(
        functools.partial(middle_kernel, devices),
        grid=grid,
        in_specs=[
            pl.BlockSpec((HALF, block, block), lambda g: (g, 0, 0)),
            pl.BlockSpec((1,) + big.shape[1:], lambda g: (g, 0, 0)),
            pl.BlockSpec((1, HALF * block, width), lambda g: (g, 0, c)),
        ]
        + [pl.BlockSpec((batch, 1, long, width), lambda g: (0, g, 0, 0))] * devices,
        out_specs=[pl.BlockSpec((batch, parts, HALF * HALF, width), lambda g: (0, 0, g, 0))] * devices
        + [pl.BlockSpec((batch, 1, HALF * block, width), lambda g: (0, g, 0, 0))],
        out_shape=(piece,) * devices + (second,),
        compiler_params=params(grid),
        cost_estimate=cost(3e9, 8e6),
    )(small, big, kern, *pieces)


def back_middle_kernel(devices, small, big, kern, second, *refs):
    pieces, outs, total = refs[:devices], refs[devices:-1], refs[-1]
    half, block = small.shape[0], small.shape[1]
    own = block // devices
    scale = kern[0].astype(F32)
    tally = None
    for b in range(second.shape[0]):
        spread = jnp.concatenate([piece[b, 0] for piece in pieces], axis=0)
        value = dot(big[0], spread)
        term = second[b, 0] * value
        tally = term if tally is None else tally + term
        weighted = (value * scale).astype(BF16)
        for i in range(0, half, 2):
            low = dot(small[i], weighted[i * block : (i + 1) * block])
            high = dot(small[i + 1], weighted[(i + 1) * block : (i + 2) * block])
            put_pair(outs, b, i * HALF, low, high, own)
    total[0] = tally


def back_middle(devices, c, width, small, big, kern, second, pieces):
    batch, parts, long, _ = pieces[0].shape
    block = small.shape[1]
    piece = jax.ShapeDtypeStruct(pieces[0].shape, BF16)
    total = jax.ShapeDtypeStruct((parts, HALF * block, width), F32)
    grid = (parts,)
    return pl.pallas_call(
        functools.partial(back_middle_kernel, devices),
        grid=grid,
        in_specs=[
            pl.BlockSpec((HALF, block, block), lambda g: (g, 0, 0)),
            pl.BlockSpec((1,) + big.shape[1:], lambda g: (g, 0, 0)),
            pl.BlockSpec((1, HALF * block, width), lambda g: (g, 0, c)),
            pl.BlockSpec((batch, 1, HALF * block, width), lambda g: (0, g, 0, 0)),
        ]
        + [pl.BlockSpec((batch, 1, long, width), lambda g: (0, g, 0, 0))] * devices,
        out_specs=[pl.BlockSpec((batch, parts, HALF * HALF, width), lambda g: (0, 0, g, 0))] * devices
        + [pl.BlockSpec((1, HALF * block, width), lambda g: (g, 0, 0))],
        out_shape=(piece,) * devices + (total,),
        compiler_params=params(grid),
        cost_estimate=cost(3e9, 8e6),
    )(small, big, kern, second, *pieces)


def gate_kernel(devices, small, weights, flat, upstream, *refs):
    outs, sloped = refs[:devices], refs[devices]
    count, block = small.shape[0], small.shape[1]
    own = block // devices
    preact = dot(flat[0], weights[...].astype(BF16))
    sigma = jax.nn.sigmoid(preact)
    swish = preact * sigma
    slope = sigma * (1.0 + preact * (1.0 - sigma))
    grad = upstream[0].astype(F32)
    sloped[0] = grad * slope
    mix_grad = (grad * swish).astype(BF16)
    for k in range(0, count, 2):
        low = dot(small[k], mix_grad[k * block : (k + 1) * block])
        high = dot(small[k + 1], mix_grad[(k + 1) * block : (k + 2) * block])
        put_pair(outs, 0, k * HALF, low, high, own)


def gate(devices, c, width, small, weights, flat, upstream):
    batch, rows, full = flat.shape
    own, block = small.shape[0], small.shape[1]
    count = 4
    piece = jax.ShapeDtypeStruct((batch, own // HALF, own * HALF, width), BF16)
    sloped = jax.ShapeDtypeStruct((batch, rows, width), F32)
    grid = (batch, own // count)
    return pl.pallas_call(
        functools.partial(gate_kernel, devices),
        grid=grid,
        in_specs=[
            pl.BlockSpec((count, block, block), lambda b, q: (q, 0, 0)),
            pl.BlockSpec((full, width), lambda b, q: (0, c)),
            pl.BlockSpec((1, count * block, full), lambda b, q: (b, q, 0)),
            pl.BlockSpec((1, count * block, width), lambda b, q: (b, q, c)),
        ],
        out_specs=[
            pl.BlockSpec((1, own // HALF, count * HALF, width), lambda b, q: (b, 0, q, 0))
        ]
        * devices
        + [pl.BlockSpec((1, count * block, width), lambda b, q: (b, q, 0))],
        out_shape=(piece,) * devices + (sloped,),
        compiler_params=params(grid),
        cost_estimate=cost(2 * batch * rows * full * width, 12e6),
    )(small, weights, flat, upstream)


def outer_kernel(devices, add, big, other, *refs):
    pieces, out = refs[:devices], refs[-1]
    spread = jnp.concatenate([piece[0, 0] for piece in pieces], axis=0)
    value = dot(big[0], spread)
    out[0] = (value + other[0] if add else value * other[0]).astype(BF16)


def outer(devices, c, width, add, big, other, before, pieces):
    batch, parts, long, _ = pieces[0].shape
    rows = big.shape[1]
    place = 0 if other.shape[2] == width else c
    full = before[0] if isinstance(before, tuple) else before.shape[2]
    grid = (parts, batch)
    operands = [big, other, *pieces]
    specs = [
        pl.BlockSpec((1,) + big.shape[1:], lambda g, b: (g, 0, 0)),
        pl.BlockSpec((1, rows, width), lambda g, b: (b, g, place)),
    ] + [pl.BlockSpec((1, 1, long, width), lambda g, b: (b, g, 0, 0))] * devices
    alias = {}
    if not isinstance(before, tuple):
        alias = {len(operands): 0}
        operands.append(before)
        specs.append(pl.BlockSpec(memory_space=pl.ANY))
    return pl.pallas_call(
        functools.partial(outer_kernel, devices, add),
        grid=grid,
        in_specs=specs,
        out_specs=pl.BlockSpec((1, rows, width), lambda g, b: (b, g, c)),
        out_shape=jax.ShapeDtypeStruct((batch, parts * rows, full), BF16),
        input_output_aliases=alias,
        compiler_params=params(grid),
        cost_estimate=cost(3e9, 6e6),
    )(*operands)


def swap(value, axis, bit):
    size = lax.axis_size(axis)
    return lax.ppermute(value, axis, [(i, i ^ bit) for i in range(size)])


def exchange(pieces):
    size = len(pieces)
    order = [size - 1, *range(1, size - 1)] if size > 1 else []
    moved = {r: swap(pieces[r], "seq", r) for r in order}
    return [pieces[0]] + [moved[r] for r in range(1, size)]


def bits_of(size):
    return [1 << k for k in range(size.bit_length() - 1)]


def has(axis, bit):
    return (lax.axis_index(axis) // bit) % 2


def halve(value, axis, bit, dim, kind):
    half = value.shape[dim] // 2
    mine = has(axis, bit)
    keep = lax.dynamic_slice_in_dim(value, mine * half, half, dim)
    send = lax.dynamic_slice_in_dim(value, (1 - mine) * half, half, dim)
    return keep + swap(send.astype(kind), axis, bit).astype(F32)


def double(value, axis, bit, dim):
    other = swap(value, axis, bit)
    mine = has(axis, bit)
    return jnp.where(
        mine == 0,
        jnp.concatenate([value, other], axis=dim),
        jnp.concatenate([other, value], axis=dim),
    )


def by_peer(value, dim):
    devices = lax.axis_size("seq")
    shape = value.shape
    for bit in bits_of(devices):
        pairs = value.reshape(
            *shape[:dim], devices // (2 * bit), 2, bit * shape[dim] // devices, *shape[dim + 1 :]
        )
        turned = jnp.flip(pairs, axis=dim + 1)
        value = jnp.where(has("seq", bit) == 0, pairs, turned).reshape(shape)
    return value


def gather_weights(gate_weight):
    devices = lax.axis_size("seq")
    sections = lax.axis_size("section")
    rows, width = gate_weight.shape
    shared = [bit for bit in (2, 1) if bit < sections and rows % (4 * 16) == 0]
    part = rows // (1 << len(shared))
    place = sum(has("section", bit) * bit for bit in shared)
    mine = lax.dynamic_slice_in_dim(gate_weight, place * part, part, 0).astype(F32)
    got = jnp.stack([mine] + [swap(mine, "seq", r) for r in range(1, devices)])
    got = by_peer(got, 0)
    if shared:
        got = double(got, "section", 1, 1)
        got = double(got, "section", 2, 1)
    return got.reshape(devices * rows, width)


def local(
    layer_input,
    grad_out,
    gate_weight,
    mix_in_right,
    mix_in_left,
    mix_out_left,
    mix_out_right,
    kernel,
):
    batch, rows, full = layer_input.shape[1:]
    own, block = mix_in_right.shape[0], mix_in_right.shape[1]
    replicas = lax.axis_size("section")
    devices = lax.axis_size("seq")
    weight_scale = 1.0 / math.sqrt(replicas * BATCH * SEQ)
    kernel_scale = 1.0 / math.sqrt(replicas * BATCH)
    chunks = 3
    width = full // chunks
    flat = layer_input[0]
    upstream = grad_out[0]
    acts = flat.reshape(batch, own, block, full)
    kern = kernel.reshape(own // HALF, HALF * block, full)

    weights = gather_weights(gate_weight)
    small_r = by_peer(mix_in_right, 1)
    small_p = by_peer(mix_out_left, 1)
    spread = [exchange(first(devices, c, width, small_r, acts)) for c in range(chunks)]
    big_li, big_qo, big_pt, big_rt, small_qt, small_lt = expand(
        devices, by_peer(mix_in_left, 2), small_p, small_r, by_peer(mix_out_right, 2)
    )
    returned, seconds = [], []
    for c in range(chunks):
        *pieces, second = middle(devices, c, width, small_p, big_li, kern, spread[c])
        returned.append(exchange(pieces))
        seconds.append(second)
    back_spread, slopes = [], []
    for c in range(chunks):
        *pieces, sloped = gate(devices, c, width, small_qt, weights, flat, upstream)
        back_spread.append(exchange(pieces))
        slopes.append(sloped)
    gate_grad = (full,)
    for c in range(chunks):
        gate_grad = outer(
            devices, c, width, False, big_qo, slopes[c], gate_grad, returned[c]
        )
    back_return, totals = [], []
    for c in range(chunks):
        *pieces, total = back_middle(
            devices, c, width, small_lt, big_pt, kern, seconds[c], back_spread[c]
        )
        back_return.append(exchange(pieces))
        totals.append(total.reshape(own * block, width))
    flat_grad = gate_grad.reshape(batch * rows, full)
    gate_part = dot_last(flat_grad, weights.astype(BF16)).reshape(batch, rows, full)
    term = dot_first(flat.reshape(batch * rows, full), flat_grad) * weight_scale

    weight_grad = term.reshape(devices, full // devices, full)
    for bit in bits_of(replicas):
        weight_grad = halve(weight_grad, "section", bit, 1, F32)
    for bit in reversed(bits_of(devices)):
        weight_grad = halve(weight_grad, "seq", bit, 0, F32)
    for bit in reversed(bits_of(replicas)):
        weight_grad = double(weight_grad, "section", bit, 1)
    weight_grad = weight_grad.reshape(full // devices, full)

    kernel_parts = []
    for total in totals:
        part = total * kernel_scale
        for bit in bits_of(replicas):
            part = halve(part, "section", bit, 0, BF16)
        part = part.astype(BF16)
        for bit in reversed(bits_of(replicas)):
            part = double(part, "section", bit, 0)
        kernel_parts.append(part)
    kernel_grad = jnp.concatenate(kernel_parts, axis=1)

    input_grad = (full,)
    for c in range(chunks):
        input_grad = outer(
            devices, c, width, True, big_rt, gate_part, input_grad, back_return[c]
        )
    return (input_grad[None], weight_grad, kernel_grad)


def forward_middle(spread, left_in, left_out, kern):
    second_mixed = contract("ija,baid->bijd", left_in, spread)
    weighted = (second_mixed * kern).astype(jnp.bfloat16)
    third_mixed = contract("ikj,bijd->bikd", left_out, weighted).astype(jnp.bfloat16)
    return (second_mixed, third_mixed)


def backward_middle(back_spread, second_mixed, left_in, left_out, kern):
    back_second = contract("ikj,bkid->bijd", left_out, back_spread)
    kernel_sum = jnp.sum(second_mixed * back_second, axis=0)
    back_weighted = (back_second * kern).astype(jnp.bfloat16)
    back_first = contract("ija,bijd->biad", left_in, back_weighted).astype(jnp.bfloat16)
    return (kernel_sum, back_first)


def local_plain(
    layer_input,
    grad_out,
    gate_weight,
    mix_in_right,
    mix_in_left,
    mix_out_left,
    mix_out_right,
    kernel,
):
    count_batch = layer_input.shape[1]
    token_rows = layer_input.shape[2]
    width = layer_input.shape[3]
    groups = mix_in_right.shape[0]
    block_size = mix_in_right.shape[1]
    replicas = lax.axis_size("section")
    kern = kernel.reshape(groups, block_size, width).astype(jnp.float32)
    acts = layer_input[0].reshape(count_batch, groups, block_size, width)
    flat_input = layer_input[0].reshape(count_batch * token_rows, width)
    upstream = grad_out[0].reshape(count_batch * token_rows, width).astype(jnp.float32)
    weights = lax.all_gather(gate_weight, "seq", axis=0, tiled=True)
    preact = jnp.dot(flat_input, weights, preferred_element_type=jnp.float32)
    sigma = jax.nn.sigmoid(preact)
    swish = preact * sigma
    slope = sigma * (1.0 + preact * (1.0 - sigma))
    mix_grad = (
        (upstream * swish).astype(jnp.bfloat16).reshape(count_batch, groups, block_size, width)
    )
    first_mixed = contract("aic,bacd->baid", mix_in_right, acts).astype(jnp.bfloat16)
    back_third = contract("kmi,bkmd->bkid", mix_out_right, mix_grad).astype(jnp.bfloat16)
    spread = lax.all_to_all(first_mixed, "seq", split_axis=2, concat_axis=1, tiled=True)
    second_mixed, third_mixed = forward_middle(spread, mix_in_left, mix_out_left, kern)
    returned = lax.all_to_all(third_mixed, "seq", split_axis=2, concat_axis=1, tiled=True)
    back_spread = lax.all_to_all(back_third, "seq", split_axis=2, concat_axis=1, tiled=True)
    kernel_sum, back_first = backward_middle(
        back_spread, second_mixed, mix_in_left, mix_out_left, kern
    )
    back_return = lax.all_to_all(back_first, "seq", split_axis=2, concat_axis=1, tiled=True)
    mixed = contract("kmi,bikd->bkmd", mix_out_right, returned).reshape(
        count_batch * token_rows, width
    )
    gate_grad = (upstream * mixed * slope).astype(jnp.bfloat16)
    gate_part = lax.dot_general(
        gate_grad, weights, (((1,), (1,)), ((), ())), preferred_element_type=jnp.float32
    )
    weight_scale = 1.0 / math.sqrt(replicas * BATCH * SEQ)
    kernel_scale = 1.0 / math.sqrt(replicas * BATCH)
    term = lax.dot_general(
        flat_input, gate_grad, (((0,), (0,)), ((), ())), preferred_element_type=jnp.float32
    )
    weight_local = lax.psum_scatter(term * weight_scale, "seq", scatter_dimension=0, tiled=True)
    weight_grad, kernel_total = lax.psum((weight_local, kernel_sum * kernel_scale), "section")
    mix_part = contract("aic,biad->bacd", mix_in_right, back_return).reshape(
        count_batch * token_rows, width
    )
    input_grad = (
        (gate_part + mix_part).astype(jnp.bfloat16).reshape(1, count_batch, token_rows, width)
    )
    kernel_grad = kernel_total.astype(jnp.bfloat16).reshape(groups * block_size, width)
    return (input_grad, weight_grad, kernel_grad)


def solution(mesh):
    placed = (
        P("section", None, "seq", None),
        P("section", None, "seq", None),
        P("seq", None),
        P("seq", None, None),
        P("seq", None, None),
        P("seq", None, None),
        P("seq", None, None),
        P("seq", None),
    )
    return jax.shard_map(
        local if 64 // mesh.shape["seq"] >= 16 else local_plain,
        mesh=mesh,
        in_specs=placed,
        out_specs=(P("section", None, "seq", None), P("seq", None), P("seq", None)),
        check_vma=False,
    )
```

```python
import functools
import math

import jax
import jax.numpy as jnp
from jax import lax
from jax.experimental import pallas as pl
from jax.experimental.pallas import tpu as pltpu
from jax.sharding import PartitionSpec as P

BATCH = 3
SEQ = 4096
HALF = 8

BF16 = jnp.bfloat16
F32 = jnp.float32


def contract(form, left, right):
    return jnp.einsum(form, left, right, preferred_element_type=jnp.float32)


def dot(left, right):
    return jnp.dot(left, right, preferred_element_type=F32)


def dot_first(left, right):
    return lax.dot_general(left, right, (((0,), (0,)), ((), ())), preferred_element_type=F32)


def dot_last(left, right):
    return lax.dot_general(left, right, (((1,), (1,)), ((), ())), preferred_element_type=F32)


def params(grid):
    return pltpu.CompilerParams(
        dimension_semantics=("arbitrary",) * len(grid), vmem_limit_bytes=56 * 1024 * 1024
    )


def cost(flops, bytes_accessed):
    return pl.CostEstimate(flops=1000, bytes_accessed=1000, transcendentals=0)


def put_pair(outs, where, low, first, second, own, columns=slice(None)):
    for r, out in enumerate(outs):
        for g in range(own // HALF):
            at = r * own + g * HALF
            rows = jnp.concatenate([first[at : at + HALF], second[at : at + HALF]], axis=0)
            out[where, g, low : low + 2 * HALF, columns] = rows.astype(BF16)


def expand_kernel(devices, left_in, left_out, right_in, right_out, right_turned, *outs):
    big_li, big_qo, big_pt, big_rt, small_qt, small_lt = outs
    own, block = left_in.shape[0], left_in.shape[1]
    wide = block * HALF
    s = lax.broadcasted_iota(jnp.int32, (block, wide), 0)
    lane = lax.broadcasted_iota(jnp.int32, (block, wide), 1)
    picks = [
        jnp.where(lane == s * HALF + t, 1.0, 0.0).astype(BF16) for t in range(HALF)
    ]
    row = lax.broadcasted_iota(jnp.int32, (block, block), 0)
    column = lax.broadcasted_iota(jnp.int32, (block, block), 1)
    same = jnp.where(row == column, 1.0, 0.0).astype(BF16)
    for p in range(own):
        g, t = divmod(p, HALF)
        rows = slice(t * block, (t + 1) * block)
        big_li[g, rows, :] = dot(left_in[p], picks[t]).astype(BF16)
        big_qo[g, rows, :] = dot(right_out[p], picks[t]).astype(BF16)
        big_pt[g, rows, :] = dot_first(left_out[p], picks[t]).astype(BF16)
        big_rt[g, rows, :] = dot_first(right_in[p], picks[t]).astype(BF16)
        small_qt[p] = dot_last(same, right_turned[p]).astype(BF16)
        small_lt[p] = dot_last(same, left_in[p]).astype(BF16)


def expand(devices, left_in, left_out, right_in, right_out, right_turned):
    own, block = left_in.shape[0], left_in.shape[1]
    big = jax.ShapeDtypeStruct((own // HALF, HALF * block, HALF * block), BF16)
    small = jax.ShapeDtypeStruct(left_in.shape, BF16)
    return pl.pallas_call(
        functools.partial(expand_kernel, devices),
        out_shape=(big,) * 4 + (small,) * 2,
        compiler_params=params(()),
        cost_estimate=cost(4e9, 8e6),
    )(left_in, left_out, right_in, right_out, right_turned)


def each(refs, devices):
    return refs if len(refs) == devices else [refs[0].at[r] for r in range(devices)]


def piece_shapes(devices, joint, batch, own, width):
    shape = (batch, own // HALF, own * HALF, width)
    if joint:
        return [jax.ShapeDtypeStruct((devices,) + shape, BF16)]
    return [jax.ShapeDtypeStruct(shape, BF16)] * devices


def piece_specs(devices, joint, block, index):
    if joint:
        return [pl.BlockSpec((devices,) + block, lambda *at: (0,) + index(*at))]
    return [pl.BlockSpec(block, index)] * devices


def first_kernel(devices, right_in, acts, *refs):
    own = right_in.shape[0]
    outs = each(refs, devices)
    for b in range(acts.shape[0]):
        for p in range(0, own, 2):
            low, high = dot(right_in[p], acts[b, p]), dot(right_in[p + 1], acts[b, p + 1])
            put_pair(outs, b, p * HALF, low, high, own)


def first(devices, width, joint, right_in, acts):
    batch, own, block, full = acts.shape
    grid = (full // width,)
    shapes = piece_shapes(devices, joint, batch, own, full)
    return pl.pallas_call(
        functools.partial(first_kernel, devices),
        grid=grid,
        in_specs=[
            pl.BlockSpec(right_in.shape, lambda c: (0, 0, 0)),
            pl.BlockSpec((batch, own, block, width), lambda c: (0, 0, 0, c)),
        ],
        out_specs=piece_specs(
            devices, joint, shapes[0].shape[-4:-1] + (width,), lambda c: (0, 0, 0, c)
        ),
        out_shape=shapes,
        compiler_params=params(grid),
        cost_estimate=cost(1e9, 1e6),
    )(right_in, acts)


def middle_kernel(devices, count, small, big, kern, *refs):
    pieces, outs, second = each(refs[:count], devices), each(refs[count:-1], devices), refs[-1]
    half, block = small.shape[0], small.shape[1]
    own = block // devices
    scale = kern[0].astype(F32)
    for b in range(second.shape[0]):
        spread = jnp.concatenate([piece[b, 0] for piece in pieces], axis=0)
        value = dot(big[0], spread)
        second[b, 0] = value
        weighted = (value * scale).astype(BF16)
        for i in range(0, half, 2):
            low = dot(small[i], weighted[i * block : (i + 1) * block])
            high = dot(small[i + 1], weighted[(i + 1) * block : (i + 2) * block])
            put_pair(outs, b, i * HALF, low, high, own)


def middle(devices, width, joint_in, joint, small, big, kern, pieces):
    batch, parts, long, full = pieces[0].shape[-4:]
    block = small.shape[1]
    second = jax.ShapeDtypeStruct((batch, parts, HALF * block, full), F32)
    grid = (parts, full // width)
    return pl.pallas_call(
        functools.partial(middle_kernel, devices, len(pieces)),
        grid=grid,
        in_specs=[
            pl.BlockSpec((HALF, block, block), lambda g, c: (g, 0, 0)),
            pl.BlockSpec((1,) + big.shape[1:], lambda g, c: (g, 0, 0)),
            pl.BlockSpec((1, HALF * block, width), lambda g, c: (g, 0, c)),
        ]
        + piece_specs(devices, joint_in, (batch, 1, long, width), lambda g, c: (0, g, 0, c)),
        out_specs=piece_specs(
            devices, joint, (batch, parts, HALF * HALF, width), lambda g, c: (0, 0, g, c)
        )
        + [pl.BlockSpec((batch, 1, HALF * block, width), lambda g, c: (0, g, 0, c))],
        out_shape=piece_shapes(devices, joint, batch, small.shape[0], full) + [second],
        compiler_params=params(grid),
        cost_estimate=cost(3e9, 8e6),
    )(small, big, kern, *pieces)


def back_middle_kernel(devices, count, small, big, kern, second, *refs):
    pieces, outs, total = each(refs[:count], devices), each(refs[count:-1], devices), refs[-1]
    half, block = small.shape[0], small.shape[1]
    own = block // devices
    scale = kern[0].astype(F32)
    tally = None
    for b in range(second.shape[0]):
        spread = jnp.concatenate([piece[b, 0] for piece in pieces], axis=0)
        value = dot(big[0], spread)
        term = second[b, 0] * value
        tally = term if tally is None else tally + term
        weighted = (value * scale).astype(BF16)
        for i in range(0, half, 2):
            low = dot(small[i], weighted[i * block : (i + 1) * block])
            high = dot(small[i + 1], weighted[(i + 1) * block : (i + 2) * block])
            put_pair(outs, b, i * HALF, low, high, own)
    total[0] = tally


def back_middle(devices, c, width, joint_in, joint, small, big, kern, second, pieces):
    batch, parts, long, _ = pieces[0].shape[-4:]
    block = small.shape[1]
    total = jax.ShapeDtypeStruct((parts, HALF * block, width), F32)
    grid = (parts,)
    return pl.pallas_call(
        functools.partial(back_middle_kernel, devices, len(pieces)),
        grid=grid,
        in_specs=[
            pl.BlockSpec((HALF, block, block), lambda g: (g, 0, 0)),
            pl.BlockSpec((1,) + big.shape[1:], lambda g: (g, 0, 0)),
            pl.BlockSpec((1, HALF * block, width), lambda g: (g, 0, c)),
            pl.BlockSpec((batch, 1, HALF * block, width), lambda g: (0, g, 0, c)),
        ]
        + piece_specs(devices, joint_in, (batch, 1, long, width), lambda g: (0, g, 0, c)),
        out_specs=piece_specs(
            devices, joint, (batch, parts, HALF * HALF, width), lambda g: (0, 0, g, 0)
        )
        + [pl.BlockSpec((1, HALF * block, width), lambda g: (g, 0, 0))],
        out_shape=piece_shapes(devices, joint, batch, small.shape[0], width) + [total],
        compiler_params=params(grid),
        cost_estimate=cost(3e9, 8e6),
    )(small, big, kern, second, *pieces)


def gate_kernel(devices, width, small, weights, flat, upstream, *refs):
    pieces, sloped = refs[:-1], refs[-1]
    block = small.shape[1]
    own = block // devices
    rows = 4 * block
    for low in range(0, flat.shape[1], rows):
        here = slice(low, low + rows)
        for columns in (slice(0, width), slice(width, 2 * width)):
            preact = dot(flat[0, here, :], weights[:, columns].astype(BF16))
            sigma = 0.5 * jnp.tanh(0.5 * preact) + 0.5
            swish = preact * sigma
            slope = sigma + swish * (1.0 - sigma)
            grad = upstream[0, here, columns].astype(F32)
            sloped[0, here, columns] = grad * slope
            mix_grad = (grad * swish).astype(BF16)
            for q in range(0, 4, 2):
                k = low // block + q
                first_product = dot(small[k], mix_grad[q * block : (q + 1) * block])
                next_product = dot(small[k + 1], mix_grad[(q + 1) * block : (q + 2) * block])
                put_pair(pieces, 0, k * HALF, first_product, next_product, own, columns)


def gate(devices, small, weights, flat, upstream):
    batch, rows, full = flat.shape
    own, block = small.shape[0], small.shape[1]
    count = own // 2
    width = full // 2
    piece = jax.ShapeDtypeStruct((batch, own // HALF, own * HALF, full), BF16)
    sloped = jax.ShapeDtypeStruct((batch, rows, full), F32)
    grid = (batch, own // count)
    part = pl.BlockSpec((1, count * block, full), lambda b, q: (b, q, 0))
    return pl.pallas_call(
        functools.partial(gate_kernel, devices, width),
        grid=grid,
        in_specs=[
            pl.BlockSpec((count, block, block), lambda b, q: (q, 0, 0)),
            pl.BlockSpec((full, full), lambda b, q: (0, 0)),
            part,
            part,
        ],
        out_specs=[
            pl.BlockSpec((1, own // HALF, count * HALF, full), lambda b, q: (b, 0, q, 0))
        ]
        * devices
        + [part],
        out_shape=(piece,) * devices + (sloped,),
        compiler_params=params(grid),
        cost_estimate=cost(14e9, 30e6),
    )(small, weights, flat, upstream)


def ending_kernel(devices, count, scale, big, sloped, weights, flat, *refs):
    pieces, part, total = each(refs[:count], devices), refs[-2], refs[-1]
    step = pl.program_id(0) * pl.num_programs(1) + pl.program_id(1)

    @pl.when(step == 0)
    def _():
        total[...] = jnp.zeros_like(total)

    spread = jnp.concatenate([piece[0, 0] for piece in pieces], axis=0)
    grad = (dot(big[0], spread) * sloped[0]).astype(BF16)
    part[0] = dot_last(grad, weights[...].astype(BF16))
    total[...] += dot_first(flat[0], grad) * scale


def ending(devices, joint, scale, big, sloped, weights, flat, pieces):
    batch, parts, long, full = pieces[0].shape[-4:]
    rows = big.shape[1]
    grid = (parts, batch)
    part = pl.BlockSpec((1, rows, full), lambda g, b: (b, g, 0))
    whole = pl.BlockSpec((full, full), lambda g, b: (0, 0))
    return pl.pallas_call(
        functools.partial(ending_kernel, devices, len(pieces), scale),
        grid=grid,
        in_specs=[pl.BlockSpec((1,) + big.shape[1:], lambda g, b: (g, 0, 0)), part, whole, part]
        + piece_specs(devices, joint, (1, 1, long, full), lambda g, b: (b, g, 0, 0)),
        out_specs=[part, whole],
        out_shape=[
            jax.ShapeDtypeStruct(sloped.shape, F32),
            jax.ShapeDtypeStruct((full, full), F32),
        ],
        compiler_params=params(grid),
        cost_estimate=cost(5e9, 8e6),
    )(big, sloped, weights, flat, *pieces)


def outer_kernel(devices, add, count, big, other, *refs):
    pieces, out = each(refs[:count], devices), refs[-1]
    for b in range(out.shape[0]):
        spread = jnp.concatenate([piece[b, 0] for piece in pieces], axis=0)
        value = dot(big[0], spread)
        out[b] = (value + other[b] if add else value * other[b]).astype(BF16)


def outer(devices, c, width, joint, add, big, other, before, pieces):
    batch, parts, long, _ = pieces[0].shape[-4:]
    rows = big.shape[1]
    grid = (parts,)
    operands = [big, other, *pieces]
    specs = [
        pl.BlockSpec((1,) + big.shape[1:], lambda g: (g, 0, 0)),
        pl.BlockSpec((batch, rows, width), lambda g: (0, g, c)),
    ] + piece_specs(devices, joint, (batch, 1, long, width), lambda g: (0, g, 0, 0))
    alias = {}
    if before is not None:
        alias = {len(operands): 0}
        operands.append(before)
        specs.append(pl.BlockSpec(memory_space=pl.ANY))
    return pl.pallas_call(
        functools.partial(outer_kernel, devices, add, len(pieces)),
        grid=grid,
        in_specs=specs,
        out_specs=pl.BlockSpec((batch, rows, width), lambda g: (0, g, c)),
        out_shape=jax.ShapeDtypeStruct(other.shape, BF16),
        input_output_aliases=alias,
        compiler_params=params(grid),
        cost_estimate=cost(5e9, 8e6),
    )(*operands)


def after(value, *earlier):
    return lax.optimization_barrier((value, *earlier))[0]


def swap(value, axis, bit):
    size = lax.axis_size(axis)
    return lax.ppermute(value, axis, [(i, i ^ bit) for i in range(size)])


def exchange(pieces):
    if len(pieces) == 1:
        return [lax.all_to_all(pieces[0], "seq", 0, 0, tiled=True)]
    size = len(pieces)
    order = [size - 1, *range(1, size - 1)] if size > 1 else []
    moved = {r: swap(pieces[r], "seq", r) for r in order}
    return [pieces[0]] + [moved[r] for r in range(1, size)]


def bits_of(size):
    return [1 << k for k in range(size.bit_length() - 1)]


def has(axis, bit):
    return (lax.axis_index(axis) // bit) % 2


def halve(value, axis, bit, dim, kind):
    half = value.shape[dim] // 2
    mine = has(axis, bit)
    keep = lax.dynamic_slice_in_dim(value, mine * half, half, dim)
    send = lax.dynamic_slice_in_dim(value, (1 - mine) * half, half, dim)
    return keep + swap(send.astype(kind), axis, bit).astype(F32)


def double(value, axis, bit, dim):
    other = swap(value, axis, bit)
    mine = has(axis, bit)
    return jnp.where(
        mine == 0,
        jnp.concatenate([value, other], axis=dim),
        jnp.concatenate([other, value], axis=dim),
    )


def by_peer(value, dim, axis="seq", unit=1):
    devices = lax.axis_size(axis) // unit
    shape = value.shape
    for bit in bits_of(devices):
        pairs = value.reshape(
            *shape[:dim], devices // (2 * bit), 2, bit * shape[dim] // devices, *shape[dim + 1 :]
        )
        turned = jnp.flip(pairs, axis=dim + 1)
        value = jnp.where(has(axis, bit * unit) == 0, pairs, turned).reshape(shape)
    return value


def scatter(value, axis, unit, dim, kind):
    peers = lax.axis_size(axis) // unit
    block = value.shape[dim] // peers
    me = lax.axis_index(axis) // unit
    total = lax.dynamic_slice_in_dim(value, me * block, block, dim)
    for r in range(1, peers):
        part = lax.dynamic_slice_in_dim(value, jnp.bitwise_xor(me, r) * block, block, dim)
        total = total + swap(part.astype(kind), axis, r * unit).astype(F32)
    return total


def collect(value, axis, unit, dim):
    peers = lax.axis_size(axis) // unit
    blocks = [value] + [swap(value, axis, r * unit) for r in range(1, peers)]
    return by_peer(jnp.concatenate(blocks, axis=dim), dim, axis, unit)


def gather_weights(gate_weight, earlier):
    devices = lax.axis_size("seq")
    sections = lax.axis_size("section")
    rows, width = gate_weight.shape
    shared = [bit for bit in (2, 1) if bit < sections and rows % (4 * 16) == 0]
    part = rows // (1 << len(shared))
    place = sum(has("section", bit) << k for k, bit in enumerate(shared))
    mine = lax.dynamic_slice_in_dim(gate_weight, place * part, part, 0).astype(F32)
    got = jnp.stack([mine] + [swap(mine, "seq", r) for r in range(1, devices)])
    got = by_peer(after(got, earlier), 0)
    for bit in shared:
        got = double(got, "section", bit, 1)
    return got.reshape(devices * rows, width)


def local(
    layer_input,
    grad_out,
    gate_weight,
    mix_in_right,
    mix_in_left,
    mix_out_left,
    mix_out_right,
    kernel,
):
    batch, rows, full = layer_input.shape[1:]
    own, block = mix_in_right.shape[0], mix_in_right.shape[1]
    replicas = lax.axis_size("section")
    devices = lax.axis_size("seq")
    weight_scale = 1.0 / math.sqrt(replicas * BATCH * SEQ)
    kernel_scale = 1.0 / math.sqrt(replicas * BATCH)
    width = full // 2
    flat = layer_input[0]
    upstream = grad_out[0]
    acts = flat.reshape(batch, own, block, full)
    kern = kernel.reshape(own // HALF, HALF * block, full)

    firsts = first(devices, width, True, mix_in_right, acts)
    spread = exchange(firsts)
    small_p = by_peer(after(mix_out_left, firsts), 1)
    right_turned = by_peer(after(mix_out_right, firsts), 2)
    big_li, big_qo, big_pt, big_rt, small_qt, small_lt = expand(
        devices, mix_in_left, small_p, mix_in_right, mix_out_right, right_turned
    )
    weights = gather_weights(after(gate_weight, firsts), big_li)
    *back_third, sloped = gate(devices, small_qt, weights, flat, upstream)
    back_spread = exchange(after(back_third, spread))
    *third, second = middle(
        devices, width, True, True, after(mix_out_left, sloped), big_li, kern, spread
    )
    returned = exchange(after(third, *back_spread))

    sixth = full // 6
    parts = ((0, 5 * sixth), (5, sixth))
    back_first, totals = [], []
    for c, wide in parts:
        sent, total = back_middle(
            devices, c, wide, False, True, after(small_lt, second, *totals), big_pt, kern, second,
            back_spread,
        )
        back_first.append(sent)
        totals.append(total)
    kernel_grad = jnp.concatenate(totals, axis=2).reshape(own * block, full) * kernel_scale
    kernel_grad = halve(kernel_grad, "section", 1, 0, BF16)
    kernel_grad = scatter(kernel_grad, "section", 2, 0, BF16).astype(BF16)
    back_first[0] = after(back_first[0], kernel_grad)
    gate_part, weight_grad = ending(
        devices, True, weight_scale, after(big_qo, kernel_grad), sloped, weights, flat, returned
    )
    weight_grad = weight_grad.reshape(devices, full // devices, full)
    weight_grad = halve(weight_grad, "section", 1, 1, BF16)
    weight_grad = scatter(weight_grad, "section", 2, 1, BF16)
    weight_grad = scatter(weight_grad, "seq", 1, 0, F32)
    kernel_grad = collect(kernel_grad, "section", 2, 0)
    kernel_grad = double(kernel_grad, "section", 1, 0)
    back_return = [exchange([after(back_first[0], *returned)])]
    back_return.append(exchange([after(back_first[1], *back_return[0], weight_grad)]))

    input_grad = None
    halves = []
    for (c, wide), arrived in zip(parts, back_return):
        input_grad = outer(
            devices, c, wide, True, True, big_rt, gate_part, input_grad, arrived
        )
        halves.append(input_grad)
    weight_grad = collect(after(weight_grad, *back_return[0]), "section", 2, 1)
    weight_grad = double(after(weight_grad, halves[0]), "section", 1, 1)
    weight_grad = weight_grad.reshape(full // devices, full)
    return (input_grad[None], weight_grad, kernel_grad)


def forward_middle(spread, left_in, left_out, kern):
    second_mixed = contract("ija,baid->bijd", left_in, spread)
    weighted = (second_mixed * kern).astype(jnp.bfloat16)
    third_mixed = contract("ikj,bijd->bikd", left_out, weighted).astype(jnp.bfloat16)
    return (second_mixed, third_mixed)


def backward_middle(back_spread, second_mixed, left_in, left_out, kern):
    back_second = contract("ikj,bkid->bijd", left_out, back_spread)
    kernel_sum = jnp.sum(second_mixed * back_second, axis=0)
    back_weighted = (back_second * kern).astype(jnp.bfloat16)
    back_first = contract("ija,bijd->biad", left_in, back_weighted).astype(jnp.bfloat16)
    return (kernel_sum, back_first)


def local_plain(
    layer_input,
    grad_out,
    gate_weight,
    mix_in_right,
    mix_in_left,
    mix_out_left,
    mix_out_right,
    kernel,
):
    count_batch = layer_input.shape[1]
    token_rows = layer_input.shape[2]
    width = layer_input.shape[3]
    groups = mix_in_right.shape[0]
    block_size = mix_in_right.shape[1]
    replicas = lax.axis_size("section")
    kern = kernel.reshape(groups, block_size, width).astype(jnp.float32)
    acts = layer_input[0].reshape(count_batch, groups, block_size, width)
    flat_input = layer_input[0].reshape(count_batch * token_rows, width)
    upstream = grad_out[0].reshape(count_batch * token_rows, width).astype(jnp.float32)
    weights = lax.all_gather(gate_weight, "seq", axis=0, tiled=True)
    preact = jnp.dot(flat_input, weights, preferred_element_type=jnp.float32)
    sigma = jax.nn.sigmoid(preact)
    swish = preact * sigma
    slope = sigma * (1.0 + preact * (1.0 - sigma))
    mix_grad = (
        (upstream * swish).astype(jnp.bfloat16).reshape(count_batch, groups, block_size, width)
    )
    first_mixed = contract("aic,bacd->baid", mix_in_right, acts).astype(jnp.bfloat16)
    back_third = contract("kmi,bkmd->bkid", mix_out_right, mix_grad).astype(jnp.bfloat16)
    spread = lax.all_to_all(first_mixed, "seq", split_axis=2, concat_axis=1, tiled=True)
    second_mixed, third_mixed = forward_middle(spread, mix_in_left, mix_out_left, kern)
    returned = lax.all_to_all(third_mixed, "seq", split_axis=2, concat_axis=1, tiled=True)
    back_spread = lax.all_to_all(back_third, "seq", split_axis=2, concat_axis=1, tiled=True)
    kernel_sum, back_first = backward_middle(
        back_spread, second_mixed, mix_in_left, mix_out_left, kern
    )
    back_return = lax.all_to_all(back_first, "seq", split_axis=2, concat_axis=1, tiled=True)
    mixed = contract("kmi,bikd->bkmd", mix_out_right, returned).reshape(
        count_batch * token_rows, width
    )
    gate_grad = (upstream * mixed * slope).astype(jnp.bfloat16)
    gate_part = lax.dot_general(
        gate_grad, weights, (((1,), (1,)), ((), ())), preferred_element_type=jnp.float32
    )
    weight_scale = 1.0 / math.sqrt(replicas * BATCH * SEQ)
    kernel_scale = 1.0 / math.sqrt(replicas * BATCH)
    term = lax.dot_general(
        flat_input, gate_grad, (((0,), (0,)), ((), ())), preferred_element_type=jnp.float32
    )
    weight_local = lax.psum_scatter(term * weight_scale, "seq", scatter_dimension=0, tiled=True)
    weight_grad, kernel_total = lax.psum((weight_local, kernel_sum * kernel_scale), "section")
    mix_part = contract("aic,biad->bacd", mix_in_right, back_return).reshape(
        count_batch * token_rows, width
    )
    input_grad = (
        (gate_part + mix_part).astype(jnp.bfloat16).reshape(1, count_batch, token_rows, width)
    )
    kernel_grad = kernel_total.astype(jnp.bfloat16).reshape(groups * block_size, width)
    return (input_grad, weight_grad, kernel_grad)


def solution(mesh):
    placed = (
        P("section", None, "seq", None),
        P("section", None, "seq", None),
        P("seq", None),
        P("seq", None, None),
        P("seq", None, None),
        P("seq", None, None),
        P("seq", None, None),
        P("seq", None),
    )
    return jax.shard_map(
        local if 64 // mesh.shape["seq"] >= 16 else local_plain,
        mesh=mesh,
        in_specs=placed,
        out_specs=(P("section", None, "seq", None), P("seq", None), P("seq", None)),
        check_vma=False,
    )
```

```python
import functools
import math

import jax
import jax.numpy as jnp
from jax import lax
from jax.experimental import pallas as pl
from jax.experimental.pallas import tpu as pltpu
from jax.sharding import PartitionSpec as P

BATCH = 3
SEQ = 4096
HALF = 8

BF16 = jnp.bfloat16
F32 = jnp.float32


def contract(form, left, right):
    return jnp.einsum(form, left, right, preferred_element_type=jnp.float32)


def dot(left, right):
    return jnp.dot(left, right, preferred_element_type=F32)


def dot_first(left, right):
    return lax.dot_general(left, right, (((0,), (0,)), ((), ())), preferred_element_type=F32)


def dot_last(left, right):
    return lax.dot_general(left, right, (((1,), (1,)), ((), ())), preferred_element_type=F32)


def params(grid):
    return pltpu.CompilerParams(
        dimension_semantics=("arbitrary",) * len(grid), vmem_limit_bytes=56 * 1024 * 1024
    )


def cost(flops, bytes_accessed):
    return pl.CostEstimate(flops=1000, bytes_accessed=1000, transcendentals=0)


def put_pair(outs, where, low, first, second, own, columns=slice(None)):
    for r, out in enumerate(outs):
        for g in range(own // HALF):
            at = r * own + g * HALF
            rows = jnp.concatenate([first[at : at + HALF], second[at : at + HALF]], axis=0)
            out[where, g, low : low + 2 * HALF, columns] = rows.astype(BF16)


def expand_kernel(devices, left_in, left_out, right_in, right_out, right_turned, *outs):
    big_li, big_qo, big_pt, big_rt, small_qt, small_lt = outs
    own, block = left_in.shape[0], left_in.shape[1]
    wide = block * HALF
    s = lax.broadcasted_iota(jnp.int32, (block, wide), 0)
    lane = lax.broadcasted_iota(jnp.int32, (block, wide), 1)
    picks = [
        jnp.where(lane == s * HALF + t, 1.0, 0.0).astype(BF16) for t in range(HALF)
    ]
    row = lax.broadcasted_iota(jnp.int32, (block, block), 0)
    column = lax.broadcasted_iota(jnp.int32, (block, block), 1)
    same = jnp.where(row == column, 1.0, 0.0).astype(BF16)
    for p in range(own):
        g, t = divmod(p, HALF)
        rows = slice(t * block, (t + 1) * block)
        big_li[g, rows, :] = dot(left_in[p], picks[t]).astype(BF16)
        big_qo[g, rows, :] = dot(right_out[p], picks[t]).astype(BF16)
        big_pt[g, rows, :] = dot_first(left_out[p], picks[t]).astype(BF16)
        big_rt[g, rows, :] = dot_first(right_in[p], picks[t]).astype(BF16)
        small_qt[p] = dot_last(same, right_turned[p]).astype(BF16)
        small_lt[p] = dot_last(same, left_in[p]).astype(BF16)


def expand(devices, left_in, left_out, right_in, right_out, right_turned):
    own, block = left_in.shape[0], left_in.shape[1]
    big = jax.ShapeDtypeStruct((own // HALF, HALF * block, HALF * block), BF16)
    small = jax.ShapeDtypeStruct(left_in.shape, BF16)
    return pl.pallas_call(
        functools.partial(expand_kernel, devices),
        out_shape=(big,) * 4 + (small,) * 2,
        compiler_params=params(()),
        cost_estimate=cost(4e9, 8e6),
    )(left_in, left_out, right_in, right_out, right_turned)


def each(refs, devices):
    return refs if len(refs) == devices else [refs[0].at[r] for r in range(devices)]


def piece_shapes(devices, joint, batch, own, width):
    shape = (batch, own // HALF, own * HALF, width)
    if joint:
        return [jax.ShapeDtypeStruct((devices,) + shape, BF16)]
    return [jax.ShapeDtypeStruct(shape, BF16)] * devices


def piece_specs(devices, joint, block, index):
    if joint:
        return [pl.BlockSpec((devices,) + block, lambda *at: (0,) + index(*at))]
    return [pl.BlockSpec(block, index)] * devices


def first_kernel(devices, right_in, acts, *refs):
    own = right_in.shape[0]
    outs = each(refs, devices)
    for b in range(acts.shape[0]):
        for p in range(0, own, 2):
            low, high = dot(right_in[p], acts[b, p]), dot(right_in[p + 1], acts[b, p + 1])
            put_pair(outs, b, p * HALF, low, high, own)


def first(devices, width, joint, right_in, acts):
    batch, own, block, full = acts.shape
    grid = (full // width,)
    shapes = piece_shapes(devices, joint, batch, own, full)
    return pl.pallas_call(
        functools.partial(first_kernel, devices),
        grid=grid,
        in_specs=[
            pl.BlockSpec(right_in.shape, lambda c: (0, 0, 0)),
            pl.BlockSpec((batch, own, block, width), lambda c: (0, 0, 0, c)),
        ],
        out_specs=piece_specs(
            devices, joint, shapes[0].shape[-4:-1] + (width,), lambda c: (0, 0, 0, c)
        ),
        out_shape=shapes,
        compiler_params=params(grid),
        cost_estimate=cost(1e9, 1e6),
    )(right_in, acts)


def middle_kernel(devices, count, small, big, kern, *refs):
    pieces, outs, second = each(refs[:count], devices), each(refs[count:-1], devices), refs[-1]
    half, block = small.shape[0], small.shape[1]
    own = block // devices
    scale = kern[0].astype(F32)
    for b in range(second.shape[0]):
        spread = jnp.concatenate([piece[b, 0] for piece in pieces], axis=0)
        value = dot(big[0], spread)
        second[b, 0] = value
        weighted = (value * scale).astype(BF16)
        for i in range(0, half, 2):
            low = dot(small[i], weighted[i * block : (i + 1) * block])
            high = dot(small[i + 1], weighted[(i + 1) * block : (i + 2) * block])
            put_pair(outs, b, i * HALF, low, high, own)


def middle(devices, width, joint_in, joint, small, big, kern, pieces):
    batch, parts, long, full = pieces[0].shape[-4:]
    block = small.shape[1]
    second = jax.ShapeDtypeStruct((batch, parts, HALF * block, full), F32)
    grid = (parts, full // width)
    return pl.pallas_call(
        functools.partial(middle_kernel, devices, len(pieces)),
        grid=grid,
        in_specs=[
            pl.BlockSpec((HALF, block, block), lambda g, c: (g, 0, 0)),
            pl.BlockSpec((1,) + big.shape[1:], lambda g, c: (g, 0, 0)),
            pl.BlockSpec((1, HALF * block, width), lambda g, c: (g, 0, c)),
        ]
        + piece_specs(devices, joint_in, (batch, 1, long, width), lambda g, c: (0, g, 0, c)),
        out_specs=piece_specs(
            devices, joint, (batch, parts, HALF * HALF, width), lambda g, c: (0, 0, g, c)
        )
        + [pl.BlockSpec((batch, 1, HALF * block, width), lambda g, c: (0, g, 0, c))],
        out_shape=piece_shapes(devices, joint, batch, small.shape[0], full) + [second],
        compiler_params=params(grid),
        cost_estimate=cost(3e9, 8e6),
    )(small, big, kern, *pieces)


def back_middle_kernel(devices, count, small, big, kern, second, *refs):
    pieces, outs, total = each(refs[:count], devices), each(refs[count:-1], devices), refs[-1]
    half, block = small.shape[0], small.shape[1]
    own = block // devices
    scale = kern[0].astype(F32)
    tally = None
    for b in range(second.shape[0]):
        spread = jnp.concatenate([piece[b, 0] for piece in pieces], axis=0)
        value = dot(big[0], spread)
        term = second[b, 0] * value
        tally = term if tally is None else tally + term
        weighted = (value * scale).astype(BF16)
        for i in range(0, half, 2):
            low = dot(small[i], weighted[i * block : (i + 1) * block])
            high = dot(small[i + 1], weighted[(i + 1) * block : (i + 2) * block])
            put_pair(outs, b, i * HALF, low, high, own)
    total[0] = tally


def back_middle(devices, c, width, joint_in, joint, small, big, kern, second, pieces):
    batch, parts, long, _ = pieces[0].shape[-4:]
    block = small.shape[1]
    total = jax.ShapeDtypeStruct((parts, HALF * block, width), F32)
    grid = (parts,)
    return pl.pallas_call(
        functools.partial(back_middle_kernel, devices, len(pieces)),
        grid=grid,
        in_specs=[
            pl.BlockSpec((HALF, block, block), lambda g: (g, 0, 0)),
            pl.BlockSpec((1,) + big.shape[1:], lambda g: (g, 0, 0)),
            pl.BlockSpec((1, HALF * block, width), lambda g: (g, 0, c)),
            pl.BlockSpec((batch, 1, HALF * block, width), lambda g: (0, g, 0, c)),
        ]
        + piece_specs(devices, joint_in, (batch, 1, long, width), lambda g: (0, g, 0, c)),
        out_specs=piece_specs(
            devices, joint, (batch, parts, HALF * HALF, width), lambda g: (0, 0, g, 0)
        )
        + [pl.BlockSpec((1, HALF * block, width), lambda g: (g, 0, 0))],
        out_shape=piece_shapes(devices, joint, batch, small.shape[0], width) + [total],
        compiler_params=params(grid),
        cost_estimate=cost(3e9, 8e6),
    )(small, big, kern, second, *pieces)


def gate_kernel(devices, width, small, weights, flat, upstream, *refs):
    pieces, sloped = refs[:-1], refs[-1]
    block = small.shape[1]
    own = block // devices
    rows = 4 * block
    for low in range(0, flat.shape[1], rows):
        here = slice(low, low + rows)
        for columns in (slice(0, width), slice(width, 2 * width)):
            preact = dot(flat[0, here, :], weights[:, columns].astype(BF16))
            sigma = 0.5 * jnp.tanh(0.5 * preact) + 0.5
            swish = preact * sigma
            slope = sigma + swish * (1.0 - sigma)
            grad = upstream[0, here, columns].astype(F32)
            sloped[0, here, columns] = grad * slope
            mix_grad = (grad * swish).astype(BF16)
            for q in range(0, 4, 2):
                k = low // block + q
                first_product = dot(small[k], mix_grad[q * block : (q + 1) * block])
                next_product = dot(small[k + 1], mix_grad[(q + 1) * block : (q + 2) * block])
                put_pair(pieces, 0, k * HALF, first_product, next_product, own, columns)


def gate(devices, small, weights, flat, upstream):
    batch, rows, full = flat.shape
    own, block = small.shape[0], small.shape[1]
    count = own // 2
    width = full // 2
    piece = jax.ShapeDtypeStruct((batch, own // HALF, own * HALF, full), BF16)
    sloped = jax.ShapeDtypeStruct((batch, rows, full), F32)
    grid = (batch, own // count)
    part = pl.BlockSpec((1, count * block, full), lambda b, q: (b, q, 0))
    return pl.pallas_call(
        functools.partial(gate_kernel, devices, width),
        grid=grid,
        in_specs=[
            pl.BlockSpec((count, block, block), lambda b, q: (q, 0, 0)),
            pl.BlockSpec((full, full), lambda b, q: (0, 0)),
            part,
            part,
        ],
        out_specs=[
            pl.BlockSpec((1, own // HALF, count * HALF, full), lambda b, q: (b, 0, q, 0))
        ]
        * devices
        + [part],
        out_shape=(piece,) * devices + (sloped,),
        compiler_params=params(grid),
        cost_estimate=cost(14e9, 30e6),
    )(small, weights, flat, upstream)


def ending_kernel(devices, count, scale, big, sloped, weights, flat, *refs):
    pieces, part, keep, send, total = each(refs[:count], devices), *refs[count:]
    steps = pl.num_programs(0) * pl.num_programs(1)
    step = pl.program_id(0) * pl.num_programs(1) + pl.program_id(1)

    @pl.when(step == 0)
    def _():
        total[...] = jnp.zeros_like(total)

    spread = jnp.concatenate([piece[0, 0] for piece in pieces], axis=0)
    grad = (dot(big[0], spread) * sloped[0]).astype(BF16)
    part[0] = dot_last(grad, weights[...].astype(BF16))
    total[...] += dot_first(flat[0], grad) * scale

    @pl.when(step == steps - 1)
    def _():
        mine = lax.axis_index("section") % 2
        rows = keep.shape[1]
        for q in range(devices):
            low = pl.multiple_of((2 * q + mine) * rows, rows)
            other = pl.multiple_of((2 * q + 1 - mine) * rows, rows)
            keep[q] = total[pl.ds(low, rows), :]
            send[q] = total[pl.ds(other, rows), :].astype(BF16)


def ending(devices, joint, scale, big, sloped, weights, flat, pieces):
    batch, parts, long, full = pieces[0].shape[-4:]
    rows = big.shape[1]
    grid = (parts, batch)
    part = pl.BlockSpec((1, rows, full), lambda g, b: (b, g, 0))
    half = (devices, full // devices // 2, full)
    return pl.pallas_call(
        functools.partial(ending_kernel, devices, len(pieces), scale),
        grid=grid,
        in_specs=[
            pl.BlockSpec((1,) + big.shape[1:], lambda g, b: (g, 0, 0)),
            part,
            pl.BlockSpec((full, full), lambda g, b: (0, 0)),
            part,
        ]
        + piece_specs(devices, joint, (1, 1, long, full), lambda g, b: (b, g, 0, 0)),
        out_specs=[part] + [pl.BlockSpec(half, lambda g, b: (0, 0, 0))] * 2,
        out_shape=[
            jax.ShapeDtypeStruct(sloped.shape, F32),
            jax.ShapeDtypeStruct(half, F32),
            jax.ShapeDtypeStruct(half, BF16),
        ],
        scratch_shapes=[pltpu.VMEM((full, full), F32)],
        compiler_params=params(grid),
        cost_estimate=cost(5e9, 8e6),
    )(big, sloped, weights, flat, *pieces)


def outer_kernel(devices, add, count, big, other, *refs):
    pieces, out = each(refs[:count], devices), refs[-1]
    for b in range(out.shape[0]):
        spread = jnp.concatenate([piece[b, 0] for piece in pieces], axis=0)
        value = dot(big[0], spread)
        out[b] = (value + other[b] if add else value * other[b]).astype(BF16)


def outer(devices, c, width, joint, add, big, other, before, pieces):
    batch, parts, long, _ = pieces[0].shape[-4:]
    rows = big.shape[1]
    grid = (parts,)
    operands = [big, other, *pieces]
    specs = [
        pl.BlockSpec((1,) + big.shape[1:], lambda g: (g, 0, 0)),
        pl.BlockSpec((batch, rows, width), lambda g: (0, g, c)),
    ] + piece_specs(devices, joint, (batch, 1, long, width), lambda g: (0, g, 0, 0))
    alias = {}
    if before is not None:
        alias = {len(operands): 0}
        operands.append(before)
        specs.append(pl.BlockSpec(memory_space=pl.ANY))
    return pl.pallas_call(
        functools.partial(outer_kernel, devices, add, len(pieces)),
        grid=grid,
        in_specs=specs,
        out_specs=pl.BlockSpec((batch, rows, width), lambda g: (0, g, c)),
        out_shape=jax.ShapeDtypeStruct(other.shape, BF16),
        input_output_aliases=alias,
        compiler_params=params(grid),
        cost_estimate=cost(5e9, 8e6),
    )(*operands)


def after(value, *earlier):
    return lax.optimization_barrier((value, *earlier))[0]


def swap(value, axis, bit):
    size = lax.axis_size(axis)
    return lax.ppermute(value, axis, [(i, i ^ bit) for i in range(size)])


def exchange(pieces):
    if len(pieces) == 1:
        return [lax.all_to_all(pieces[0], "seq", 0, 0, tiled=True)]
    size = len(pieces)
    order = [size - 1, *range(1, size - 1)] if size > 1 else []
    moved = {r: swap(pieces[r], "seq", r) for r in order}
    return [pieces[0]] + [moved[r] for r in range(1, size)]


def bits_of(size):
    return [1 << k for k in range(size.bit_length() - 1)]


def has(axis, bit):
    return (lax.axis_index(axis) // bit) % 2


def halve(value, axis, bit, dim, kind):
    half = value.shape[dim] // 2
    mine = has(axis, bit)
    keep = lax.dynamic_slice_in_dim(value, mine * half, half, dim)
    send = lax.dynamic_slice_in_dim(value, (1 - mine) * half, half, dim)
    return keep + swap(send.astype(kind), axis, bit).astype(F32)


def double(value, axis, bit, dim, other=None):
    other = swap(value, axis, bit) if other is None else other
    mine = has(axis, bit)
    return jnp.where(
        mine == 0,
        jnp.concatenate([value, other], axis=dim),
        jnp.concatenate([other, value], axis=dim),
    )


def by_peer(value, dim, axis="seq", unit=1):
    devices = lax.axis_size(axis) // unit
    shape = value.shape
    for bit in bits_of(devices):
        pairs = value.reshape(
            *shape[:dim], devices // (2 * bit), 2, bit * shape[dim] // devices, *shape[dim + 1 :]
        )
        turned = jnp.flip(pairs, axis=dim + 1)
        value = jnp.where(has(axis, bit * unit) == 0, pairs, turned).reshape(shape)
    return value


def scatter(value, axis, unit, dim, kind):
    peers = lax.axis_size(axis) // unit
    block = value.shape[dim] // peers
    me = lax.axis_index(axis) // unit
    total = lax.dynamic_slice_in_dim(value, me * block, block, dim)
    for r in range(1, peers):
        part = lax.dynamic_slice_in_dim(value, jnp.bitwise_xor(me, r) * block, block, dim)
        total = total + swap(part.astype(kind), axis, r * unit).astype(F32)
    return total


def blocks_of(value, axis, unit):
    peers = lax.axis_size(axis) // unit
    return [value] + [swap(value, axis, r * unit) for r in range(1, peers)]


def collect(blocks, axis, unit, dim):
    return by_peer(jnp.concatenate(blocks, axis=dim), dim, axis, unit)


def gather_weights(gate_weight, earlier):
    devices = lax.axis_size("seq")
    sections = lax.axis_size("section")
    rows, width = gate_weight.shape
    shared = [bit for bit in (2, 1) if bit < sections and rows % (4 * 16) == 0]
    part = rows // (1 << len(shared))
    place = sum(has("section", bit) << k for k, bit in enumerate(shared))
    mine = lax.dynamic_slice_in_dim(gate_weight, place * part, part, 0).astype(F32)
    got = jnp.stack([mine] + [swap(mine, "seq", r) for r in range(1, devices)])
    got = by_peer(after(got, earlier), 0)
    for bit in shared:
        got = double(got, "section", bit, 1)
    return got.reshape(devices * rows, width)


def local(
    layer_input,
    grad_out,
    gate_weight,
    mix_in_right,
    mix_in_left,
    mix_out_left,
    mix_out_right,
    kernel,
):
    batch, rows, full = layer_input.shape[1:]
    own, block = mix_in_right.shape[0], mix_in_right.shape[1]
    replicas = lax.axis_size("section")
    devices = lax.axis_size("seq")
    weight_scale = 1.0 / math.sqrt(replicas * BATCH * SEQ)
    kernel_scale = 1.0 / math.sqrt(replicas * BATCH)
    width = full // 2
    flat = layer_input[0]
    upstream = grad_out[0]
    acts = flat.reshape(batch, own, block, full)
    kern = kernel.reshape(own // HALF, HALF * block, full)

    firsts = first(devices, width, True, mix_in_right, acts)
    spread = exchange(firsts)
    small_p = by_peer(after(mix_out_left, firsts), 1)
    right_turned = by_peer(after(mix_out_right, firsts), 2)
    big_li, big_qo, big_pt, big_rt, small_qt, small_lt = expand(
        devices, mix_in_left, small_p, mix_in_right, mix_out_right, right_turned
    )
    weights = gather_weights(after(gate_weight, firsts), big_li)
    *back_third, sloped = gate(devices, small_qt, weights, flat, upstream)
    back_spread = exchange(back_third)
    *third, second = middle(
        devices, width, True, True, after(mix_out_left, sloped), big_li, kern, spread
    )
    returned = exchange(after(third, *back_spread))

    third_width = full // 3
    parts = ((0, 2 * third_width), (2, third_width))
    back_first, totals = [], []
    for c, wide in parts:
        sent, total = back_middle(
            devices, c, wide, False, True, after(small_lt, second, *totals), big_pt, kern, second,
            back_spread,
        )
        back_first.append(sent)
        totals.append(total)
    kernel_grad = jnp.concatenate(totals, axis=2).reshape(own * block, full) * kernel_scale
    kernel_grad = halve(kernel_grad, "section", 1, 0, BF16)
    kernel_grad = scatter(kernel_grad, "section", 2, 0, BF16).astype(BF16)
    back_first[0] = after(back_first[0], kernel_grad)
    gate_part, keep, sent = ending(
        devices, True, weight_scale, after(big_qo, kernel_grad), sloped, weights, flat, returned
    )
    kernel_blocks = blocks_of(kernel_grad, "section", 2)
    weight_grad = keep + swap(after(sent, *kernel_blocks), "section", 1).astype(F32)
    kernel_grad = collect(after(kernel_blocks, weight_grad), "section", 2, 0)
    kernel_other = swap(kernel_grad, "section", 1)
    weight_grad = scatter(weight_grad, "section", 2, 1, BF16)
    back_return = [exchange([after(back_first[0], *returned)])]
    back_return.append(
        exchange([after(back_first[1], *back_return[0], weight_grad, kernel_other)])
    )
    weight_grad = scatter(weight_grad, "seq", 1, 0, F32)

    kernel_other = after(kernel_other, *back_return[0])
    kernel_grad = double(kernel_grad, "section", 1, 0, kernel_other)

    input_grad = None
    halves = []
    for (c, wide), arrived in zip(parts, back_return):
        input_grad = outer(
            devices, c, wide, True, True, big_rt, gate_part, input_grad, arrived
        )
        halves.append(input_grad)
    weight_blocks = blocks_of(after(weight_grad, *back_return[0]), "section", 2)
    weight_grad = collect(weight_blocks, "section", 2, 1)
    weight_grad = double(after(weight_grad, halves[0]), "section", 1, 1)
    weight_grad = weight_grad.reshape(full // devices, full)
    return (input_grad[None], weight_grad, kernel_grad)


def forward_middle(spread, left_in, left_out, kern):
    second_mixed = contract("ija,baid->bijd", left_in, spread)
    weighted = (second_mixed * kern).astype(jnp.bfloat16)
    third_mixed = contract("ikj,bijd->bikd", left_out, weighted).astype(jnp.bfloat16)
    return (second_mixed, third_mixed)


def backward_middle(back_spread, second_mixed, left_in, left_out, kern):
    back_second = contract("ikj,bkid->bijd", left_out, back_spread)
    kernel_sum = jnp.sum(second_mixed * back_second, axis=0)
    back_weighted = (back_second * kern).astype(jnp.bfloat16)
    back_first = contract("ija,bijd->biad", left_in, back_weighted).astype(jnp.bfloat16)
    return (kernel_sum, back_first)


def local_plain(
    layer_input,
    grad_out,
    gate_weight,
    mix_in_right,
    mix_in_left,
    mix_out_left,
    mix_out_right,
    kernel,
):
    count_batch = layer_input.shape[1]
    token_rows = layer_input.shape[2]
    width = layer_input.shape[3]
    groups = mix_in_right.shape[0]
    block_size = mix_in_right.shape[1]
    replicas = lax.axis_size("section")
    kern = kernel.reshape(groups, block_size, width).astype(jnp.float32)
    acts = layer_input[0].reshape(count_batch, groups, block_size, width)
    flat_input = layer_input[0].reshape(count_batch * token_rows, width)
    upstream = grad_out[0].reshape(count_batch * token_rows, width).astype(jnp.float32)
    weights = lax.all_gather(gate_weight, "seq", axis=0, tiled=True)
    preact = jnp.dot(flat_input, weights, preferred_element_type=jnp.float32)
    sigma = jax.nn.sigmoid(preact)
    swish = preact * sigma
    slope = sigma * (1.0 + preact * (1.0 - sigma))
    mix_grad = (
        (upstream * swish).astype(jnp.bfloat16).reshape(count_batch, groups, block_size, width)
    )
    first_mixed = contract("aic,bacd->baid", mix_in_right, acts).astype(jnp.bfloat16)
    back_third = contract("kmi,bkmd->bkid", mix_out_right, mix_grad).astype(jnp.bfloat16)
    spread = lax.all_to_all(first_mixed, "seq", split_axis=2, concat_axis=1, tiled=True)
    second_mixed, third_mixed = forward_middle(spread, mix_in_left, mix_out_left, kern)
    returned = lax.all_to_all(third_mixed, "seq", split_axis=2, concat_axis=1, tiled=True)
    back_spread = lax.all_to_all(back_third, "seq", split_axis=2, concat_axis=1, tiled=True)
    kernel_sum, back_first = backward_middle(
        back_spread, second_mixed, mix_in_left, mix_out_left, kern
    )
    back_return = lax.all_to_all(back_first, "seq", split_axis=2, concat_axis=1, tiled=True)
    mixed = contract("kmi,bikd->bkmd", mix_out_right, returned).reshape(
        count_batch * token_rows, width
    )
    gate_grad = (upstream * mixed * slope).astype(jnp.bfloat16)
    gate_part = lax.dot_general(
        gate_grad, weights, (((1,), (1,)), ((), ())), preferred_element_type=jnp.float32
    )
    weight_scale = 1.0 / math.sqrt(replicas * BATCH * SEQ)
    kernel_scale = 1.0 / math.sqrt(replicas * BATCH)
    term = lax.dot_general(
        flat_input, gate_grad, (((0,), (0,)), ((), ())), preferred_element_type=jnp.float32
    )
    weight_local = lax.psum_scatter(term * weight_scale, "seq", scatter_dimension=0, tiled=True)
    weight_grad, kernel_total = lax.psum((weight_local, kernel_sum * kernel_scale), "section")
    mix_part = contract("aic,biad->bacd", mix_in_right, back_return).reshape(
        count_batch * token_rows, width
    )
    input_grad = (
        (gate_part + mix_part).astype(jnp.bfloat16).reshape(1, count_batch, token_rows, width)
    )
    kernel_grad = kernel_total.astype(jnp.bfloat16).reshape(groups * block_size, width)
    return (input_grad, weight_grad, kernel_grad)


def solution(mesh):
    placed = (
        P("section", None, "seq", None),
        P("section", None, "seq", None),
        P("seq", None),
        P("seq", None, None),
        P("seq", None, None),
        P("seq", None, None),
        P("seq", None, None),
        P("seq", None),
    )
    return jax.shard_map(
        local if 64 // mesh.shape["seq"] >= 16 else local_plain,
        mesh=mesh,
        in_specs=placed,
        out_specs=(P("section", None, "seq", None), P("seq", None), P("seq", None)),
        check_vma=False,
    )
```

```python
import functools
import math

import jax
import jax.numpy as jnp
from jax import lax
from jax.experimental import pallas as pl
from jax.experimental.pallas import tpu as pltpu
from jax.sharding import PartitionSpec as P

BATCH = 3
SEQ = 4096
HALF = 8

BF16 = jnp.bfloat16
F32 = jnp.float32


def contract(form, left, right):
    return jnp.einsum(form, left, right, preferred_element_type=jnp.float32)


def dot(left, right):
    return jnp.dot(left, right, preferred_element_type=F32)


def dot_first(left, right):
    return lax.dot_general(left, right, (((0,), (0,)), ((), ())), preferred_element_type=F32)


def dot_last(left, right):
    return lax.dot_general(left, right, (((1,), (1,)), ((), ())), preferred_element_type=F32)


def params(grid):
    return pltpu.CompilerParams(
        dimension_semantics=("arbitrary",) * len(grid), vmem_limit_bytes=56 * 1024 * 1024
    )


def cost(flops, bytes_accessed):
    return pl.CostEstimate(flops=1000, bytes_accessed=1000, transcendentals=0)


def put_pair(outs, where, low, first, second, own, columns=slice(None)):
    for r, out in enumerate(outs):
        for g in range(own // HALF):
            at = r * own + g * HALF
            rows = jnp.concatenate([first[at : at + HALF], second[at : at + HALF]], axis=0)
            out[where, g, low : low + 2 * HALF, columns] = rows.astype(BF16)


def expand_kernel(devices, left_in, left_out, right_in, right_out, right_turned, *outs):
    big_li, big_qo, big_pt, big_rt, small_qt, small_lt = outs
    own, block = left_in.shape[0], left_in.shape[1]
    wide = block * HALF
    s = lax.broadcasted_iota(jnp.int32, (block, wide), 0)
    lane = lax.broadcasted_iota(jnp.int32, (block, wide), 1)
    picks = [
        jnp.where(lane == s * HALF + t, 1.0, 0.0).astype(BF16) for t in range(HALF)
    ]
    row = lax.broadcasted_iota(jnp.int32, (block, block), 0)
    column = lax.broadcasted_iota(jnp.int32, (block, block), 1)
    same = jnp.where(row == column, 1.0, 0.0).astype(BF16)
    for p in range(own):
        g, t = divmod(p, HALF)
        rows = slice(t * block, (t + 1) * block)
        big_li[g, rows, :] = dot(left_in[p], picks[t]).astype(BF16)
        big_qo[g, rows, :] = dot(right_out[p], picks[t]).astype(BF16)
        big_pt[g, rows, :] = dot_first(left_out[p], picks[t]).astype(BF16)
        big_rt[g, rows, :] = dot_first(right_in[p], picks[t]).astype(BF16)
        small_qt[p] = dot_last(same, right_turned[p]).astype(BF16)
        small_lt[p] = dot_last(same, left_in[p]).astype(BF16)


def expand(devices, left_in, left_out, right_in, right_out, right_turned):
    own, block = left_in.shape[0], left_in.shape[1]
    big = jax.ShapeDtypeStruct((own // HALF, HALF * block, HALF * block), BF16)
    small = jax.ShapeDtypeStruct(left_in.shape, BF16)
    return pl.pallas_call(
        functools.partial(expand_kernel, devices),
        out_shape=(big,) * 4 + (small,) * 2,
        compiler_params=params(()),
        cost_estimate=cost(4e9, 8e6),
    )(left_in, left_out, right_in, right_out, right_turned)


def each(refs, devices):
    return refs if len(refs) == devices else [refs[0].at[r] for r in range(devices)]


def piece_shapes(devices, joint, batch, own, width):
    shape = (batch, own // HALF, own * HALF, width)
    if joint:
        return [jax.ShapeDtypeStruct((devices,) + shape, BF16)]
    return [jax.ShapeDtypeStruct(shape, BF16)] * devices


def piece_specs(devices, joint, block, index):
    if joint:
        return [pl.BlockSpec((devices,) + block, lambda *at: (0,) + index(*at))]
    return [pl.BlockSpec(block, index)] * devices


def first_kernel(devices, right_in, acts, *refs):
    own = right_in.shape[0]
    outs = each(refs, devices)
    for b in range(acts.shape[0]):
        for p in range(0, own, 2):
            low, high = dot(right_in[p], acts[b, p]), dot(right_in[p + 1], acts[b, p + 1])
            put_pair(outs, b, p * HALF, low, high, own)


def first(devices, width, joint, right_in, acts):
    batch, own, block, full = acts.shape
    grid = (full // width,)
    shapes = piece_shapes(devices, joint, batch, own, full)
    return pl.pallas_call(
        functools.partial(first_kernel, devices),
        grid=grid,
        in_specs=[
            pl.BlockSpec(right_in.shape, lambda c: (0, 0, 0)),
            pl.BlockSpec((batch, own, block, width), lambda c: (0, 0, 0, c)),
        ],
        out_specs=piece_specs(
            devices, joint, shapes[0].shape[-4:-1] + (width,), lambda c: (0, 0, 0, c)
        ),
        out_shape=shapes,
        compiler_params=params(grid),
        cost_estimate=cost(1e9, 1e6),
    )(right_in, acts)


def middle_kernel(devices, count, small, big, kern, *refs):
    pieces, outs, second = each(refs[:count], devices), each(refs[count:-1], devices), refs[-1]
    half, block = small.shape[0], small.shape[1]
    own = block // devices
    scale = kern[0].astype(F32)
    for b in range(second.shape[0]):
        spread = jnp.concatenate([piece[b, 0] for piece in pieces], axis=0)
        value = dot(big[0], spread)
        second[b, 0] = value
        weighted = (value * scale).astype(BF16)
        for i in range(0, half, 2):
            low = dot(small[i], weighted[i * block : (i + 1) * block])
            high = dot(small[i + 1], weighted[(i + 1) * block : (i + 2) * block])
            put_pair(outs, b, i * HALF, low, high, own)


def middle(devices, width, joint_in, joint, small, big, kern, pieces):
    batch, parts, long, full = pieces[0].shape[-4:]
    block = small.shape[1]
    second = jax.ShapeDtypeStruct((batch, parts, HALF * block, full), F32)
    grid = (parts, full // width)
    return pl.pallas_call(
        functools.partial(middle_kernel, devices, len(pieces)),
        grid=grid,
        in_specs=[
            pl.BlockSpec((HALF, block, block), lambda g, c: (g, 0, 0)),
            pl.BlockSpec((1,) + big.shape[1:], lambda g, c: (g, 0, 0)),
            pl.BlockSpec((1, HALF * block, width), lambda g, c: (g, 0, c)),
        ]
        + piece_specs(devices, joint_in, (batch, 1, long, width), lambda g, c: (0, g, 0, c)),
        out_specs=piece_specs(
            devices, joint, (batch, parts, HALF * HALF, width), lambda g, c: (0, 0, g, c)
        )
        + [pl.BlockSpec((batch, 1, HALF * block, width), lambda g, c: (0, g, 0, c))],
        out_shape=piece_shapes(devices, joint, batch, small.shape[0], full) + [second],
        compiler_params=params(grid),
        cost_estimate=cost(3e9, 8e6),
    )(small, big, kern, *pieces)


def back_middle_kernel(devices, count, small, big, kern, second, *refs):
    pieces, outs, total = each(refs[:count], devices), each(refs[count:-1], devices), refs[-1]
    half, block = small.shape[0], small.shape[1]
    own = block // devices
    scale = kern[0].astype(F32)
    tally = None
    for b in range(second.shape[0]):
        spread = jnp.concatenate([piece[b, 0] for piece in pieces], axis=0)
        value = dot(big[0], spread)
        term = second[b, 0] * value
        tally = term if tally is None else tally + term
        weighted = (value * scale).astype(BF16)
        for i in range(0, half, 2):
            low = dot(small[i], weighted[i * block : (i + 1) * block])
            high = dot(small[i + 1], weighted[(i + 1) * block : (i + 2) * block])
            put_pair(outs, b, i * HALF, low, high, own)
    total[0] = tally


def back_middle(devices, c, width, joint_in, joint, small, big, kern, second, pieces):
    batch, parts, long, _ = pieces[0].shape[-4:]
    block = small.shape[1]
    total = jax.ShapeDtypeStruct((parts, HALF * block, width), F32)
    grid = (parts,)
    return pl.pallas_call(
        functools.partial(back_middle_kernel, devices, len(pieces)),
        grid=grid,
        in_specs=[
            pl.BlockSpec((HALF, block, block), lambda g: (g, 0, 0)),
            pl.BlockSpec((1,) + big.shape[1:], lambda g: (g, 0, 0)),
            pl.BlockSpec((1, HALF * block, width), lambda g: (g, 0, c)),
            pl.BlockSpec((batch, 1, HALF * block, width), lambda g: (0, g, 0, c)),
        ]
        + piece_specs(devices, joint_in, (batch, 1, long, width), lambda g: (0, g, 0, c)),
        out_specs=piece_specs(
            devices, joint, (batch, parts, HALF * HALF, width), lambda g: (0, 0, g, 0)
        )
        + [pl.BlockSpec((1, HALF * block, width), lambda g: (g, 0, 0))],
        out_shape=piece_shapes(devices, joint, batch, small.shape[0], width) + [total],
        compiler_params=params(grid),
        cost_estimate=cost(3e9, 8e6),
    )(small, big, kern, second, *pieces)


def gate_kernel(devices, width, small, weights, flat, upstream, *refs):
    pieces, sloped = refs[:-1], refs[-1]
    block = small.shape[1]
    own = block // devices
    rows = 4 * block
    for low in range(0, flat.shape[1], rows):
        here = slice(low, low + rows)
        for columns in (slice(0, width), slice(width, 2 * width)):
            preact = dot(flat[0, here, :], weights[:, columns].astype(BF16))
            sigma = 0.5 * jnp.tanh(0.5 * preact) + 0.5
            swish = preact * sigma
            slope = sigma + swish * (1.0 - sigma)
            grad = upstream[0, here, columns].astype(F32)
            sloped[0, here, columns] = grad * slope
            mix_grad = (grad * swish).astype(BF16)
            for q in range(0, 4, 2):
                k = low // block + q
                first_product = dot(small[k], mix_grad[q * block : (q + 1) * block])
                next_product = dot(small[k + 1], mix_grad[(q + 1) * block : (q + 2) * block])
                put_pair(pieces, 0, k * HALF, first_product, next_product, own, columns)


def gate(devices, small, weights, flat, upstream):
    batch, rows, full = flat.shape
    own, block = small.shape[0], small.shape[1]
    count = own // 2
    width = full // 2
    piece = jax.ShapeDtypeStruct((batch, own // HALF, own * HALF, full), BF16)
    sloped = jax.ShapeDtypeStruct((batch, rows, full), F32)
    grid = (batch, own // count)
    part = pl.BlockSpec((1, count * block, full), lambda b, q: (b, q, 0))
    return pl.pallas_call(
        functools.partial(gate_kernel, devices, width),
        grid=grid,
        in_specs=[
            pl.BlockSpec((count, block, block), lambda b, q: (q, 0, 0)),
            pl.BlockSpec((full, full), lambda b, q: (0, 0)),
            part,
            part,
        ],
        out_specs=[
            pl.BlockSpec((1, own // HALF, count * HALF, full), lambda b, q: (b, 0, q, 0))
        ]
        * devices
        + [part],
        out_shape=(piece,) * devices + (sloped,),
        compiler_params=params(grid),
        cost_estimate=cost(14e9, 30e6),
    )(small, weights, flat, upstream)


def ending_kernel(devices, count, scale, big, sloped, weights, flat, *refs):
    pieces, part, keep, send, total = each(refs[:count], devices), *refs[count:]
    steps = pl.num_programs(0) * pl.num_programs(1)
    step = pl.program_id(0) * pl.num_programs(1) + pl.program_id(1)

    @pl.when(step == 0)
    def _():
        total[...] = jnp.zeros_like(total)

    spread = jnp.concatenate([piece[0, 0] for piece in pieces], axis=0)
    grad = (dot(big[0], spread) * sloped[0]).astype(BF16)
    part[0] = dot_last(grad, weights[...].astype(BF16))
    total[...] += dot_first(flat[0], grad) * scale

    @pl.when(step == steps - 1)
    def _():
        mine = lax.axis_index("section") % 2
        rows = keep.shape[1]
        for q in range(devices):
            low = pl.multiple_of((2 * q + mine) * rows, rows)
            other = pl.multiple_of((2 * q + 1 - mine) * rows, rows)
            keep[q] = total[pl.ds(low, rows), :]
            send[q] = total[pl.ds(other, rows), :].astype(BF16)


def ending(devices, joint, scale, big, sloped, weights, flat, pieces):
    batch, parts, long, full = pieces[0].shape[-4:]
    rows = big.shape[1]
    grid = (parts, batch)
    part = pl.BlockSpec((1, rows, full), lambda g, b: (b, g, 0))
    half = (devices, full // devices // 2, full)
    return pl.pallas_call(
        functools.partial(ending_kernel, devices, len(pieces), scale),
        grid=grid,
        in_specs=[
            pl.BlockSpec((1,) + big.shape[1:], lambda g, b: (g, 0, 0)),
            part,
            pl.BlockSpec((full, full), lambda g, b: (0, 0)),
            part,
        ]
        + piece_specs(devices, joint, (1, 1, long, full), lambda g, b: (b, g, 0, 0)),
        out_specs=[part] + [pl.BlockSpec(half, lambda g, b: (0, 0, 0))] * 2,
        out_shape=[
            jax.ShapeDtypeStruct(sloped.shape, F32),
            jax.ShapeDtypeStruct(half, F32),
            jax.ShapeDtypeStruct(half, BF16),
        ],
        scratch_shapes=[pltpu.VMEM((full, full), F32)],
        compiler_params=params(grid),
        cost_estimate=cost(5e9, 8e6),
    )(big, sloped, weights, flat, *pieces)


def outer_kernel(devices, add, count, big, other, *refs):
    pieces, out = each(refs[:count], devices), refs[-1]
    for b in range(out.shape[0]):
        spread = jnp.concatenate([piece[b, 0] for piece in pieces], axis=0)
        value = dot(big[0], spread)
        out[b] = (value + other[b] if add else value * other[b]).astype(BF16)


def outer(devices, c, width, joint, add, big, other, before, pieces):
    batch, parts, long, _ = pieces[0].shape[-4:]
    rows = big.shape[1]
    grid = (parts,)
    operands = [big, other, *pieces]
    specs = [
        pl.BlockSpec((1,) + big.shape[1:], lambda g: (g, 0, 0)),
        pl.BlockSpec((batch, rows, width), lambda g: (0, g, c)),
    ] + piece_specs(devices, joint, (batch, 1, long, width), lambda g: (0, g, 0, 0))
    alias = {}
    if before is not None:
        alias = {len(operands): 0}
        operands.append(before)
        specs.append(pl.BlockSpec(memory_space=pl.ANY))
    return pl.pallas_call(
        functools.partial(outer_kernel, devices, add, len(pieces)),
        grid=grid,
        in_specs=specs,
        out_specs=pl.BlockSpec((batch, rows, width), lambda g: (0, g, c)),
        out_shape=jax.ShapeDtypeStruct(other.shape, BF16),
        input_output_aliases=alias,
        compiler_params=params(grid),
        cost_estimate=cost(5e9, 8e6),
    )(*operands)


def after(value, *earlier):
    return lax.optimization_barrier((value, *earlier))[0]


def swap(value, axis, bit):
    size = lax.axis_size(axis)
    return lax.ppermute(value, axis, [(i, i ^ bit) for i in range(size)])


def exchange(pieces):
    if len(pieces) == 1:
        return [lax.all_to_all(pieces[0], "seq", 0, 0, tiled=True)]
    size = len(pieces)
    order = [size - 1, *range(1, size - 1)] if size > 1 else []
    moved = {r: swap(pieces[r], "seq", r) for r in order}
    return [pieces[0]] + [moved[r] for r in range(1, size)]


def bits_of(size):
    return [1 << k for k in range(size.bit_length() - 1)]


def has(axis, bit):
    return (lax.axis_index(axis) // bit) % 2


def halve(value, axis, bit, dim, kind):
    half = value.shape[dim] // 2
    mine = has(axis, bit)
    keep = lax.dynamic_slice_in_dim(value, mine * half, half, dim)
    send = lax.dynamic_slice_in_dim(value, (1 - mine) * half, half, dim)
    return keep + swap(send.astype(kind), axis, bit).astype(F32)


def double(value, axis, bit, dim, other=None):
    other = swap(value, axis, bit) if other is None else other
    mine = has(axis, bit)
    return jnp.where(
        mine == 0,
        jnp.concatenate([value, other], axis=dim),
        jnp.concatenate([other, value], axis=dim),
    )


def by_peer(value, dim, axis="seq", unit=1):
    devices = lax.axis_size(axis) // unit
    shape = value.shape
    for bit in bits_of(devices):
        pairs = value.reshape(
            *shape[:dim], devices // (2 * bit), 2, bit * shape[dim] // devices, *shape[dim + 1 :]
        )
        turned = jnp.flip(pairs, axis=dim + 1)
        value = jnp.where(has(axis, bit * unit) == 0, pairs, turned).reshape(shape)
    return value


def scatter(value, axis, unit, dim, kind, earlier=()):
    peers = lax.axis_size(axis) // unit
    block = value.shape[dim] // peers
    me = lax.axis_index(axis) // unit
    total = lax.dynamic_slice_in_dim(value, me * block, block, dim)
    for r in range(1, peers):
        part = lax.dynamic_slice_in_dim(value, jnp.bitwise_xor(me, r) * block, block, dim)
        moved = swap(part.astype(kind), axis, r * unit)
        total = total + (after(moved, *earlier) if earlier else moved).astype(F32)
    return total


def blocks_of(value, axis, unit):
    peers = lax.axis_size(axis) // unit
    return [value] + [swap(value, axis, r * unit) for r in range(1, peers)]


def collect(blocks, axis, unit, dim):
    return by_peer(jnp.concatenate(blocks, axis=dim), dim, axis, unit)


def gather_weights(gate_weight, earlier):
    devices = lax.axis_size("seq")
    sections = lax.axis_size("section")
    rows, width = gate_weight.shape
    shared = [bit for bit in (2, 1) if bit < sections and rows % (4 * 16) == 0]
    part = rows // (1 << len(shared))
    place = sum(has("section", bit) << k for k, bit in enumerate(shared))
    mine = lax.dynamic_slice_in_dim(gate_weight, place * part, part, 0).astype(F32)
    got = jnp.stack([mine] + [swap(mine, "seq", r) for r in range(1, devices)])
    got = by_peer(after(got, earlier), 0)
    for bit in shared:
        got = double(got, "section", bit, 1)
    return got.reshape(devices * rows, width)


def local(
    layer_input,
    grad_out,
    gate_weight,
    mix_in_right,
    mix_in_left,
    mix_out_left,
    mix_out_right,
    kernel,
):
    batch, rows, full = layer_input.shape[1:]
    own, block = mix_in_right.shape[0], mix_in_right.shape[1]
    replicas = lax.axis_size("section")
    devices = lax.axis_size("seq")
    weight_scale = 1.0 / math.sqrt(replicas * BATCH * SEQ)
    kernel_scale = 1.0 / math.sqrt(replicas * BATCH)
    width = full // 2
    flat = layer_input[0]
    upstream = grad_out[0]
    acts = flat.reshape(batch, own, block, full)
    kern = kernel.reshape(own // HALF, HALF * block, full)

    firsts = first(devices, width, True, mix_in_right, acts)
    spread = exchange(firsts)
    small_p = by_peer(after(mix_out_left, firsts), 1)
    right_turned = by_peer(after(mix_out_right, firsts), 2)
    big_li, big_qo, big_pt, big_rt, small_qt, small_lt = expand(
        devices, mix_in_left, small_p, mix_in_right, mix_out_right, right_turned
    )
    weights = gather_weights(after(gate_weight, firsts), big_li)
    *back_third, sloped = gate(devices, small_qt, weights, flat, upstream)
    back_spread = exchange(back_third)
    *third, second = middle(
        devices, width, True, True, after(mix_out_left, sloped), big_li, kern, spread
    )
    returned = exchange(after(third, *back_spread))

    third_width = full // 3
    parts = ((0, 2 * third_width), (2, third_width))
    back_first, totals = [], []
    for c, wide in parts:
        sent, total = back_middle(
            devices, c, wide, False, True, after(small_lt, second, *totals), big_pt, kern, second,
            back_spread,
        )
        back_first.append(sent)
        totals.append(total)
    kernel_grad = jnp.concatenate(totals, axis=2).reshape(own * block, full) * kernel_scale
    kernel_grad = halve(kernel_grad, "section", 1, 0, BF16)
    kernel_grad = scatter(kernel_grad, "section", 2, 0, BF16).astype(BF16)
    back_first[0] = after(back_first[0], kernel_grad)
    gate_part, keep, sent = ending(
        devices, True, weight_scale, after(big_qo, kernel_grad), sloped, weights, flat, returned
    )
    kernel_blocks = blocks_of(kernel_grad, "section", 2)
    kernel_grad = collect(after(kernel_blocks, sent), "section", 2, 0)
    moved = swap(after(sent, *kernel_blocks), "section", 1)
    weight_grad = keep + after(moved, kernel_grad).astype(F32)
    kernel_grad = double(kernel_grad, "section", 1, 0)
    weight_grad = scatter(weight_grad, "section", 2, 1, BF16, [kernel_grad])
    back_return = [exchange([after(back_first[0], *returned)])]
    back_return.append(
        exchange([after(back_first[1], *back_return[0], weight_grad, kernel_grad)])
    )
    weight_grad = scatter(weight_grad, "seq", 1, 0, F32)

    input_grad = None
    halves = []
    for (c, wide), arrived in zip(parts, back_return):
        input_grad = outer(
            devices, c, wide, True, True, big_rt, gate_part, input_grad, arrived
        )
        halves.append(input_grad)
    weight_blocks = blocks_of(after(weight_grad, *back_return[0]), "section", 2)
    weight_grad = collect(weight_blocks, "section", 2, 1)
    weight_grad = double(after(weight_grad, halves[0]), "section", 1, 1)
    weight_grad = weight_grad.reshape(full // devices, full)
    return (input_grad[None], weight_grad, kernel_grad)


def forward_middle(spread, left_in, left_out, kern):
    second_mixed = contract("ija,baid->bijd", left_in, spread)
    weighted = (second_mixed * kern).astype(jnp.bfloat16)
    third_mixed = contract("ikj,bijd->bikd", left_out, weighted).astype(jnp.bfloat16)
    return (second_mixed, third_mixed)


def backward_middle(back_spread, second_mixed, left_in, left_out, kern):
    back_second = contract("ikj,bkid->bijd", left_out, back_spread)
    kernel_sum = jnp.sum(second_mixed * back_second, axis=0)
    back_weighted = (back_second * kern).astype(jnp.bfloat16)
    back_first = contract("ija,bijd->biad", left_in, back_weighted).astype(jnp.bfloat16)
    return (kernel_sum, back_first)


def local_plain(
    layer_input,
    grad_out,
    gate_weight,
    mix_in_right,
    mix_in_left,
    mix_out_left,
    mix_out_right,
    kernel,
):
    count_batch = layer_input.shape[1]
    token_rows = layer_input.shape[2]
    width = layer_input.shape[3]
    groups = mix_in_right.shape[0]
    block_size = mix_in_right.shape[1]
    replicas = lax.axis_size("section")
    kern = kernel.reshape(groups, block_size, width).astype(jnp.float32)
    acts = layer_input[0].reshape(count_batch, groups, block_size, width)
    flat_input = layer_input[0].reshape(count_batch * token_rows, width)
    upstream = grad_out[0].reshape(count_batch * token_rows, width).astype(jnp.float32)
    weights = lax.all_gather(gate_weight, "seq", axis=0, tiled=True)
    preact = jnp.dot(flat_input, weights, preferred_element_type=jnp.float32)
    sigma = jax.nn.sigmoid(preact)
    swish = preact * sigma
    slope = sigma * (1.0 + preact * (1.0 - sigma))
    mix_grad = (
        (upstream * swish).astype(jnp.bfloat16).reshape(count_batch, groups, block_size, width)
    )
    first_mixed = contract("aic,bacd->baid", mix_in_right, acts).astype(jnp.bfloat16)
    back_third = contract("kmi,bkmd->bkid", mix_out_right, mix_grad).astype(jnp.bfloat16)
    spread = lax.all_to_all(first_mixed, "seq", split_axis=2, concat_axis=1, tiled=True)
    second_mixed, third_mixed = forward_middle(spread, mix_in_left, mix_out_left, kern)
    returned = lax.all_to_all(third_mixed, "seq", split_axis=2, concat_axis=1, tiled=True)
    back_spread = lax.all_to_all(back_third, "seq", split_axis=2, concat_axis=1, tiled=True)
    kernel_sum, back_first = backward_middle(
        back_spread, second_mixed, mix_in_left, mix_out_left, kern
    )
    back_return = lax.all_to_all(back_first, "seq", split_axis=2, concat_axis=1, tiled=True)
    mixed = contract("kmi,bikd->bkmd", mix_out_right, returned).reshape(
        count_batch * token_rows, width
    )
    gate_grad = (upstream * mixed * slope).astype(jnp.bfloat16)
    gate_part = lax.dot_general(
        gate_grad, weights, (((1,), (1,)), ((), ())), preferred_element_type=jnp.float32
    )
    weight_scale = 1.0 / math.sqrt(replicas * BATCH * SEQ)
    kernel_scale = 1.0 / math.sqrt(replicas * BATCH)
    term = lax.dot_general(
        flat_input, gate_grad, (((0,), (0,)), ((), ())), preferred_element_type=jnp.float32
    )
    weight_local = lax.psum_scatter(term * weight_scale, "seq", scatter_dimension=0, tiled=True)
    weight_grad, kernel_total = lax.psum((weight_local, kernel_sum * kernel_scale), "section")
    mix_part = contract("aic,biad->bacd", mix_in_right, back_return).reshape(
        count_batch * token_rows, width
    )
    input_grad = (
        (gate_part + mix_part).astype(jnp.bfloat16).reshape(1, count_batch, token_rows, width)
    )
    kernel_grad = kernel_total.astype(jnp.bfloat16).reshape(groups * block_size, width)
    return (input_grad, weight_grad, kernel_grad)


def solution(mesh):
    placed = (
        P("section", None, "seq", None),
        P("section", None, "seq", None),
        P("seq", None),
        P("seq", None, None),
        P("seq", None, None),
        P("seq", None, None),
        P("seq", None, None),
        P("seq", None),
    )
    return jax.shard_map(
        local if 64 // mesh.shape["seq"] >= 16 else local_plain,
        mesh=mesh,
        in_specs=placed,
        out_specs=(P("section", None, "seq", None), P("seq", None), P("seq", None)),
        check_vma=False,
    )
```

```python
import functools
import math

import jax
import jax.numpy as jnp
from jax import lax
from jax.experimental import pallas as pl
from jax.experimental.pallas import tpu as pltpu
from jax.sharding import PartitionSpec as P

BATCH = 3
SEQ = 4096
HALF = 8

BF16 = jnp.bfloat16
F32 = jnp.float32


def contract(form, left, right):
    return jnp.einsum(form, left, right, preferred_element_type=jnp.float32)


def dot(left, right):
    return jnp.dot(left, right, preferred_element_type=F32)


def dot_first(left, right):
    return lax.dot_general(left, right, (((0,), (0,)), ((), ())), preferred_element_type=F32)


def dot_last(left, right):
    return lax.dot_general(left, right, (((1,), (1,)), ((), ())), preferred_element_type=F32)


def params(grid):
    return pltpu.CompilerParams(
        dimension_semantics=("arbitrary",) * len(grid), vmem_limit_bytes=56 * 1024 * 1024
    )


def cost(flops, bytes_accessed):
    return pl.CostEstimate(flops=1000, bytes_accessed=1000, transcendentals=0)


def put_pair(outs, where, low, first, second, own, columns=slice(None)):
    for r, out in enumerate(outs):
        for g in range(own // HALF):
            at = r * own + g * HALF
            rows = jnp.concatenate([first[at : at + HALF], second[at : at + HALF]], axis=0)
            out[where, g, low : low + 2 * HALF, columns] = rows.astype(BF16)


def expand_kernel(devices, left_in, left_out, right_in, right_out, right_turned, *outs):
    big_li, big_qo, big_pt, big_rt, small_qt, small_lt = outs
    own, block = left_in.shape[0], left_in.shape[1]
    wide = block * HALF
    s = lax.broadcasted_iota(jnp.int32, (block, wide), 0)
    lane = lax.broadcasted_iota(jnp.int32, (block, wide), 1)
    picks = [
        jnp.where(lane == s * HALF + t, 1.0, 0.0).astype(BF16) for t in range(HALF)
    ]
    row = lax.broadcasted_iota(jnp.int32, (block, block), 0)
    column = lax.broadcasted_iota(jnp.int32, (block, block), 1)
    same = jnp.where(row == column, 1.0, 0.0).astype(BF16)
    for p in range(own):
        g, t = divmod(p, HALF)
        rows = slice(t * block, (t + 1) * block)
        big_li[g, rows, :] = dot(left_in[p], picks[t]).astype(BF16)
        big_qo[g, rows, :] = dot(right_out[p], picks[t]).astype(BF16)
        big_pt[g, rows, :] = dot_first(left_out[p], picks[t]).astype(BF16)
        big_rt[g, rows, :] = dot_first(right_in[p], picks[t]).astype(BF16)
        small_qt[p] = dot_last(same, right_turned[p]).astype(BF16)
        small_lt[p] = dot_last(same, left_in[p]).astype(BF16)


def expand(devices, left_in, left_out, right_in, right_out, right_turned):
    own, block = left_in.shape[0], left_in.shape[1]
    big = jax.ShapeDtypeStruct((own // HALF, HALF * block, HALF * block), BF16)
    small = jax.ShapeDtypeStruct(left_in.shape, BF16)
    return pl.pallas_call(
        functools.partial(expand_kernel, devices),
        out_shape=(big,) * 4 + (small,) * 2,
        compiler_params=params(()),
        cost_estimate=cost(4e9, 8e6),
    )(left_in, left_out, right_in, right_out, right_turned)


def each(refs, devices):
    return refs if len(refs) == devices else [refs[0].at[r] for r in range(devices)]


def piece_shapes(devices, joint, batch, own, width):
    shape = (batch, own // HALF, own * HALF, width)
    if joint:
        return [jax.ShapeDtypeStruct((devices,) + shape, BF16)]
    return [jax.ShapeDtypeStruct(shape, BF16)] * devices


def piece_specs(devices, joint, block, index):
    if joint:
        return [pl.BlockSpec((devices,) + block, lambda *at: (0,) + index(*at))]
    return [pl.BlockSpec(block, index)] * devices


def first_kernel(devices, right_in, acts, *refs):
    own = right_in.shape[0]
    outs = each(refs, devices)
    for b in range(acts.shape[0]):
        for p in range(0, own, 2):
            low, high = dot(right_in[p], acts[b, p]), dot(right_in[p + 1], acts[b, p + 1])
            put_pair(outs, b, p * HALF, low, high, own)


def first(devices, width, joint, right_in, acts):
    batch, own, block, full = acts.shape
    grid = (full // width,)
    shapes = piece_shapes(devices, joint, batch, own, full)
    return pl.pallas_call(
        functools.partial(first_kernel, devices),
        grid=grid,
        in_specs=[
            pl.BlockSpec(right_in.shape, lambda c: (0, 0, 0)),
            pl.BlockSpec((batch, own, block, width), lambda c: (0, 0, 0, c)),
        ],
        out_specs=piece_specs(
            devices, joint, shapes[0].shape[-4:-1] + (width,), lambda c: (0, 0, 0, c)
        ),
        out_shape=shapes,
        compiler_params=params(grid),
        cost_estimate=cost(1e9, 1e6),
    )(right_in, acts)


def middle_kernel(devices, count, small, big, kern, *refs):
    pieces, outs, second = each(refs[:count], devices), each(refs[count:-1], devices), refs[-1]
    half, block = small.shape[0], small.shape[1]
    own = block // devices
    scale = kern[0].astype(F32)
    for b in range(second.shape[0]):
        spread = jnp.concatenate([piece[b, 0] for piece in pieces], axis=0)
        value = dot(big[0], spread)
        second[b, 0] = value
        weighted = (value * scale).astype(BF16)
        for i in range(0, half, 2):
            low = dot(small[i], weighted[i * block : (i + 1) * block])
            high = dot(small[i + 1], weighted[(i + 1) * block : (i + 2) * block])
            put_pair(outs, b, i * HALF, low, high, own)


def middle(devices, width, joint_in, joint, small, big, kern, pieces):
    batch, parts, long, full = pieces[0].shape[-4:]
    block = small.shape[1]
    second = jax.ShapeDtypeStruct((batch, parts, HALF * block, full), F32)
    grid = (parts, full // width)
    return pl.pallas_call(
        functools.partial(middle_kernel, devices, len(pieces)),
        grid=grid,
        in_specs=[
            pl.BlockSpec((HALF, block, block), lambda g, c: (g, 0, 0)),
            pl.BlockSpec((1,) + big.shape[1:], lambda g, c: (g, 0, 0)),
            pl.BlockSpec((1, HALF * block, width), lambda g, c: (g, 0, c)),
        ]
        + piece_specs(devices, joint_in, (batch, 1, long, width), lambda g, c: (0, g, 0, c)),
        out_specs=piece_specs(
            devices, joint, (batch, parts, HALF * HALF, width), lambda g, c: (0, 0, g, c)
        )
        + [pl.BlockSpec((batch, 1, HALF * block, width), lambda g, c: (0, g, 0, c))],
        out_shape=piece_shapes(devices, joint, batch, small.shape[0], full) + [second],
        compiler_params=params(grid),
        cost_estimate=cost(3e9, 8e6),
    )(small, big, kern, *pieces)


def back_middle_kernel(devices, count, small, big, kern, second, *refs):
    pieces, outs, total = each(refs[:count], devices), each(refs[count:-1], devices), refs[-1]
    half, block = small.shape[0], small.shape[1]
    own = block // devices
    scale = kern[0].astype(F32)
    tally = None
    for b in range(second.shape[0]):
        spread = jnp.concatenate([piece[b, 0] for piece in pieces], axis=0)
        value = dot(big[0], spread)
        term = second[b, 0] * value
        tally = term if tally is None else tally + term
        weighted = (value * scale).astype(BF16)
        for i in range(0, half, 2):
            low = dot(small[i], weighted[i * block : (i + 1) * block])
            high = dot(small[i + 1], weighted[(i + 1) * block : (i + 2) * block])
            put_pair(outs, b, i * HALF, low, high, own)
    total[0] = tally


def back_middle(devices, c, width, joint_in, joint, small, big, kern, second, pieces):
    batch, parts, long, _ = pieces[0].shape[-4:]
    block = small.shape[1]
    total = jax.ShapeDtypeStruct((parts, HALF * block, width), F32)
    grid = (parts,)
    return pl.pallas_call(
        functools.partial(back_middle_kernel, devices, len(pieces)),
        grid=grid,
        in_specs=[
            pl.BlockSpec((HALF, block, block), lambda g: (g, 0, 0)),
            pl.BlockSpec((1,) + big.shape[1:], lambda g: (g, 0, 0)),
            pl.BlockSpec((1, HALF * block, width), lambda g: (g, 0, c)),
            pl.BlockSpec((batch, 1, HALF * block, width), lambda g: (0, g, 0, c)),
        ]
        + piece_specs(devices, joint_in, (batch, 1, long, width), lambda g: (0, g, 0, c)),
        out_specs=piece_specs(
            devices, joint, (batch, parts, HALF * HALF, width), lambda g: (0, 0, g, 0)
        )
        + [pl.BlockSpec((1, HALF * block, width), lambda g: (g, 0, 0))],
        out_shape=piece_shapes(devices, joint, batch, small.shape[0], width) + [total],
        compiler_params=params(grid),
        cost_estimate=cost(3e9, 8e6),
    )(small, big, kern, second, *pieces)


def gate_kernel(devices, width, small, weights, flat, upstream, *refs):
    pieces, sloped = refs[:-1], refs[-1]
    block = small.shape[1]
    own = block // devices
    rows = 4 * block
    for low in range(0, flat.shape[1], rows):
        here = slice(low, low + rows)
        for columns in (slice(0, width), slice(width, 2 * width)):
            preact = dot(flat[0, here, :], weights[:, columns].astype(BF16))
            sigma = 0.5 * jnp.tanh(0.5 * preact) + 0.5
            swish = preact * sigma
            slope = sigma + swish * (1.0 - sigma)
            grad = upstream[0, here, columns].astype(F32)
            sloped[0, here, columns] = grad * slope
            mix_grad = (grad * swish).astype(BF16)
            for q in range(0, 4, 2):
                k = low // block + q
                first_product = dot(small[k], mix_grad[q * block : (q + 1) * block])
                next_product = dot(small[k + 1], mix_grad[(q + 1) * block : (q + 2) * block])
                put_pair(pieces, 0, k * HALF, first_product, next_product, own, columns)


def gate(devices, small, weights, flat, upstream):
    batch, rows, full = flat.shape
    own, block = small.shape[0], small.shape[1]
    count = own // 2
    width = full // 2
    piece = jax.ShapeDtypeStruct((batch, own // HALF, own * HALF, full), BF16)
    sloped = jax.ShapeDtypeStruct((batch, rows, full), F32)
    grid = (batch, own // count)
    part = pl.BlockSpec((1, count * block, full), lambda b, q: (b, q, 0))
    return pl.pallas_call(
        functools.partial(gate_kernel, devices, width),
        grid=grid,
        in_specs=[
            pl.BlockSpec((count, block, block), lambda b, q: (q, 0, 0)),
            pl.BlockSpec((full, full), lambda b, q: (0, 0)),
            part,
            part,
        ],
        out_specs=[
            pl.BlockSpec((1, own // HALF, count * HALF, full), lambda b, q: (b, 0, q, 0))
        ]
        * devices
        + [part],
        out_shape=(piece,) * devices + (sloped,),
        compiler_params=params(grid),
        cost_estimate=cost(14e9, 30e6),
    )(small, weights, flat, upstream)


def ending_kernel(devices, count, scale, big, sloped, weights, flat, *refs):
    pieces, part, keep, send, total = each(refs[:count], devices), *refs[count:]
    steps = pl.num_programs(0) * pl.num_programs(1)
    step = pl.program_id(0) * pl.num_programs(1) + pl.program_id(1)

    @pl.when(step == 0)
    def _():
        total[...] = jnp.zeros_like(total)

    spread = jnp.concatenate([piece[0, 0] for piece in pieces], axis=0)
    grad = (dot(big[0], spread) * sloped[0]).astype(BF16)
    part[0] = dot_last(grad, weights[...].astype(BF16))
    total[...] += dot_first(flat[0], grad) * scale

    @pl.when(step == steps - 1)
    def _():
        mine = lax.axis_index("section") % 2
        rows = keep.shape[1]
        for q in range(devices):
            low = pl.multiple_of((2 * q + mine) * rows, rows)
            other = pl.multiple_of((2 * q + 1 - mine) * rows, rows)
            keep[q] = total[pl.ds(low, rows), :]
            send[q] = total[pl.ds(other, rows), :].astype(BF16)


def ending(devices, joint, scale, big, sloped, weights, flat, pieces):
    batch, parts, long, full = pieces[0].shape[-4:]
    rows = big.shape[1]
    grid = (parts, batch)
    part = pl.BlockSpec((1, rows, full), lambda g, b: (b, g, 0))
    half = (devices, full // devices // 2, full)
    return pl.pallas_call(
        functools.partial(ending_kernel, devices, len(pieces), scale),
        grid=grid,
        in_specs=[
            pl.BlockSpec((1,) + big.shape[1:], lambda g, b: (g, 0, 0)),
            part,
            pl.BlockSpec((full, full), lambda g, b: (0, 0)),
            part,
        ]
        + piece_specs(devices, joint, (1, 1, long, full), lambda g, b: (b, g, 0, 0)),
        out_specs=[part] + [pl.BlockSpec(half, lambda g, b: (0, 0, 0))] * 2,
        out_shape=[
            jax.ShapeDtypeStruct(sloped.shape, F32),
            jax.ShapeDtypeStruct(half, F32),
            jax.ShapeDtypeStruct(half, BF16),
        ],
        scratch_shapes=[pltpu.VMEM((full, full), F32)],
        compiler_params=params(grid),
        cost_estimate=cost(5e9, 8e6),
    )(big, sloped, weights, flat, *pieces)


def outer_kernel(devices, add, count, big, other, *refs):
    pieces, out = each(refs[:count], devices), refs[-1]
    for b in range(out.shape[0]):
        spread = jnp.concatenate([piece[b, 0] for piece in pieces], axis=0)
        value = dot(big[0], spread)
        out[b] = (value + other[b] if add else value * other[b]).astype(BF16)


def outer(devices, c, width, joint, add, big, other, before, pieces):
    batch, parts, long, _ = pieces[0].shape[-4:]
    rows = big.shape[1]
    grid = (parts,)
    operands = [big, other, *pieces]
    specs = [
        pl.BlockSpec((1,) + big.shape[1:], lambda g: (g, 0, 0)),
        pl.BlockSpec((batch, rows, width), lambda g: (0, g, c)),
    ] + piece_specs(devices, joint, (batch, 1, long, width), lambda g: (0, g, 0, 0))
    alias = {}
    if before is not None:
        alias = {len(operands): 0}
        operands.append(before)
        specs.append(pl.BlockSpec(memory_space=pl.ANY))
    return pl.pallas_call(
        functools.partial(outer_kernel, devices, add, len(pieces)),
        grid=grid,
        in_specs=specs,
        out_specs=pl.BlockSpec((batch, rows, width), lambda g: (0, g, c)),
        out_shape=jax.ShapeDtypeStruct(other.shape, BF16),
        input_output_aliases=alias,
        compiler_params=params(grid),
        cost_estimate=cost(5e9, 8e6),
    )(*operands)


def after(value, *earlier):
    return lax.optimization_barrier((value, *earlier))[0]


def swap(value, axis, bit):
    size = lax.axis_size(axis)
    return lax.ppermute(value, axis, [(i, i ^ bit) for i in range(size)])


def exchange(pieces):
    if len(pieces) == 1:
        return [lax.all_to_all(pieces[0], "seq", 0, 0, tiled=True)]
    size = len(pieces)
    order = [size - 1, *range(1, size - 1)] if size > 1 else []
    moved = {r: swap(pieces[r], "seq", r) for r in order}
    return [pieces[0]] + [moved[r] for r in range(1, size)]


def bits_of(size):
    return [1 << k for k in range(size.bit_length() - 1)]


def has(axis, bit):
    return (lax.axis_index(axis) // bit) % 2


def halve(value, axis, bit, dim, kind):
    half = value.shape[dim] // 2
    mine = has(axis, bit)
    keep = lax.dynamic_slice_in_dim(value, mine * half, half, dim)
    send = lax.dynamic_slice_in_dim(value, (1 - mine) * half, half, dim)
    return keep + swap(send.astype(kind), axis, bit).astype(F32)


def double(value, axis, bit, dim, other=None):
    other = swap(value, axis, bit) if other is None else other
    mine = has(axis, bit)
    return jnp.where(
        mine == 0,
        jnp.concatenate([value, other], axis=dim),
        jnp.concatenate([other, value], axis=dim),
    )


def by_peer(value, dim, axis="seq", unit=1):
    devices = lax.axis_size(axis) // unit
    shape = value.shape
    for bit in bits_of(devices):
        pairs = value.reshape(
            *shape[:dim], devices // (2 * bit), 2, bit * shape[dim] // devices, *shape[dim + 1 :]
        )
        turned = jnp.flip(pairs, axis=dim + 1)
        value = jnp.where(has(axis, bit * unit) == 0, pairs, turned).reshape(shape)
    return value


def scatter(value, axis, unit, dim, kind, earlier=()):
    peers = lax.axis_size(axis) // unit
    block = value.shape[dim] // peers
    me = lax.axis_index(axis) // unit
    total = lax.dynamic_slice_in_dim(value, me * block, block, dim)
    for r in range(1, peers):
        part = lax.dynamic_slice_in_dim(value, jnp.bitwise_xor(me, r) * block, block, dim)
        moved = swap(part.astype(kind), axis, r * unit)
        total = total + (after(moved, *earlier) if earlier else moved).astype(F32)
    return total


def blocks_of(value, axis, unit):
    peers = lax.axis_size(axis) // unit
    return [value] + [swap(value, axis, r * unit) for r in range(1, peers)]


def collect(blocks, axis, unit, dim):
    return by_peer(jnp.concatenate(blocks, axis=dim), dim, axis, unit)


def gather_weights(gate_weight, earlier):
    devices = lax.axis_size("seq")
    sections = lax.axis_size("section")
    rows, width = gate_weight.shape
    shared = [bit for bit in (2, 1) if bit < sections and rows % (4 * 16) == 0]
    part = rows // (1 << len(shared))
    place = sum(has("section", bit) << k for k, bit in enumerate(shared))
    mine = lax.dynamic_slice_in_dim(gate_weight, place * part, part, 0).astype(F32)
    got = jnp.stack([mine] + [swap(mine, "seq", r) for r in range(1, devices)])
    got = by_peer(after(got, earlier), 0)
    for bit in shared:
        got = double(got, "section", bit, 1)
    return got.reshape(devices * rows, width)


def local(
    layer_input,
    grad_out,
    gate_weight,
    mix_in_right,
    mix_in_left,
    mix_out_left,
    mix_out_right,
    kernel,
):
    batch, rows, full = layer_input.shape[1:]
    own, block = mix_in_right.shape[0], mix_in_right.shape[1]
    replicas = lax.axis_size("section")
    devices = lax.axis_size("seq")
    weight_scale = 1.0 / math.sqrt(replicas * BATCH * SEQ)
    kernel_scale = 1.0 / math.sqrt(replicas * BATCH)
    width = full // 2
    flat = layer_input[0]
    upstream = grad_out[0]
    acts = flat.reshape(batch, own, block, full)
    kern = kernel.reshape(own // HALF, HALF * block, full)

    firsts = first(devices, width, True, mix_in_right, acts)
    spread = exchange(firsts)
    small_p = by_peer(after(mix_out_left, firsts), 1)
    right_turned = by_peer(after(mix_out_right, firsts), 2)
    big_li, big_qo, big_pt, big_rt, small_qt, small_lt = expand(
        devices, mix_in_left, small_p, mix_in_right, mix_out_right, right_turned
    )
    weights = gather_weights(after(gate_weight, firsts), big_li)
    *back_third, sloped = gate(devices, small_qt, weights, flat, upstream)
    back_spread = exchange(back_third)
    *third, second = middle(
        devices, width, True, True, after(mix_out_left, sloped), big_li, kern, spread
    )
    returned = exchange(after(third, *back_spread))

    sixth = full // 6
    parts = ((0, 5 * sixth), (5, sixth))
    back_first, totals = [], []
    for c, wide in parts:
        sent, total = back_middle(
            devices, c, wide, False, True, after(small_lt, second, *totals), big_pt, kern, second,
            back_spread,
        )
        back_first.append(sent)
        totals.append(total)
    kernel_grad = jnp.concatenate(totals, axis=2).reshape(own * block, full) * kernel_scale
    kernel_grad = halve(kernel_grad, "section", 1, 0, BF16)
    kernel_grad = scatter(kernel_grad, "section", 2, 0, BF16).astype(BF16)
    back_first[0] = after(back_first[0], kernel_grad)
    gate_part, keep, sent = ending(
        devices, True, weight_scale, after(big_qo, kernel_grad), sloped, weights, flat, returned
    )
    kernel_blocks = blocks_of(kernel_grad, "section", 2)
    kernel_grad = collect(after(kernel_blocks, sent), "section", 2, 0)
    moved = swap(after(sent, *kernel_blocks), "section", 1)
    weight_grad = keep + after(moved, kernel_grad).astype(F32)
    kernel_grad = double(kernel_grad, "section", 1, 0)
    weight_grad = scatter(weight_grad, "section", 2, 1, BF16, [kernel_grad])
    back_return = [exchange([after(back_first[0], *returned)])]
    back_return.append(
        exchange([after(back_first[1], *back_return[0], weight_grad, kernel_grad)])
    )
    weight_grad = scatter(weight_grad, "seq", 1, 0, F32)

    input_grad = None
    halves = []
    for (c, wide), arrived in zip(parts, back_return):
        input_grad = outer(
            devices, c, wide, True, True, big_rt, gate_part, input_grad, arrived
        )
        halves.append(input_grad)
    weight_blocks = blocks_of(after(weight_grad, *back_return[0]), "section", 2)
    weight_grad = collect(weight_blocks, "section", 2, 1)
    weight_grad = double(after(weight_grad, halves[0]), "section", 1, 1)
    weight_grad = weight_grad.reshape(full // devices, full)
    return (input_grad[None], weight_grad, kernel_grad)


def forward_middle(spread, left_in, left_out, kern):
    second_mixed = contract("ija,baid->bijd", left_in, spread)
    weighted = (second_mixed * kern).astype(jnp.bfloat16)
    third_mixed = contract("ikj,bijd->bikd", left_out, weighted).astype(jnp.bfloat16)
    return (second_mixed, third_mixed)


def backward_middle(back_spread, second_mixed, left_in, left_out, kern):
    back_second = contract("ikj,bkid->bijd", left_out, back_spread)
    kernel_sum = jnp.sum(second_mixed * back_second, axis=0)
    back_weighted = (back_second * kern).astype(jnp.bfloat16)
    back_first = contract("ija,bijd->biad", left_in, back_weighted).astype(jnp.bfloat16)
    return (kernel_sum, back_first)


def local_plain(
    layer_input,
    grad_out,
    gate_weight,
    mix_in_right,
    mix_in_left,
    mix_out_left,
    mix_out_right,
    kernel,
):
    count_batch = layer_input.shape[1]
    token_rows = layer_input.shape[2]
    width = layer_input.shape[3]
    groups = mix_in_right.shape[0]
    block_size = mix_in_right.shape[1]
    replicas = lax.axis_size("section")
    kern = kernel.reshape(groups, block_size, width).astype(jnp.float32)
    acts = layer_input[0].reshape(count_batch, groups, block_size, width)
    flat_input = layer_input[0].reshape(count_batch * token_rows, width)
    upstream = grad_out[0].reshape(count_batch * token_rows, width).astype(jnp.float32)
    weights = lax.all_gather(gate_weight, "seq", axis=0, tiled=True)
    preact = jnp.dot(flat_input, weights, preferred_element_type=jnp.float32)
    sigma = jax.nn.sigmoid(preact)
    swish = preact * sigma
    slope = sigma * (1.0 + preact * (1.0 - sigma))
    mix_grad = (
        (upstream * swish).astype(jnp.bfloat16).reshape(count_batch, groups, block_size, width)
    )
    first_mixed = contract("aic,bacd->baid", mix_in_right, acts).astype(jnp.bfloat16)
    back_third = contract("kmi,bkmd->bkid", mix_out_right, mix_grad).astype(jnp.bfloat16)
    spread = lax.all_to_all(first_mixed, "seq", split_axis=2, concat_axis=1, tiled=True)
    second_mixed, third_mixed = forward_middle(spread, mix_in_left, mix_out_left, kern)
    returned = lax.all_to_all(third_mixed, "seq", split_axis=2, concat_axis=1, tiled=True)
    back_spread = lax.all_to_all(back_third, "seq", split_axis=2, concat_axis=1, tiled=True)
    kernel_sum, back_first = backward_middle(
        back_spread, second_mixed, mix_in_left, mix_out_left, kern
    )
    back_return = lax.all_to_all(back_first, "seq", split_axis=2, concat_axis=1, tiled=True)
    mixed = contract("kmi,bikd->bkmd", mix_out_right, returned).reshape(
        count_batch * token_rows, width
    )
    gate_grad = (upstream * mixed * slope).astype(jnp.bfloat16)
    gate_part = lax.dot_general(
        gate_grad, weights, (((1,), (1,)), ((), ())), preferred_element_type=jnp.float32
    )
    weight_scale = 1.0 / math.sqrt(replicas * BATCH * SEQ)
    kernel_scale = 1.0 / math.sqrt(replicas * BATCH)
    term = lax.dot_general(
        flat_input, gate_grad, (((0,), (0,)), ((), ())), preferred_element_type=jnp.float32
    )
    weight_local = lax.psum_scatter(term * weight_scale, "seq", scatter_dimension=0, tiled=True)
    weight_grad, kernel_total = lax.psum((weight_local, kernel_sum * kernel_scale), "section")
    mix_part = contract("aic,biad->bacd", mix_in_right, back_return).reshape(
        count_batch * token_rows, width
    )
    input_grad = (
        (gate_part + mix_part).astype(jnp.bfloat16).reshape(1, count_batch, token_rows, width)
    )
    kernel_grad = kernel_total.astype(jnp.bfloat16).reshape(groups * block_size, width)
    return (input_grad, weight_grad, kernel_grad)


def solution(mesh):
    placed = (
        P("section", None, "seq", None),
        P("section", None, "seq", None),
        P("seq", None),
        P("seq", None, None),
        P("seq", None, None),
        P("seq", None, None),
        P("seq", None, None),
        P("seq", None),
    )
    return jax.shard_map(
        local if 64 // mesh.shape["seq"] >= 16 else local_plain,
        mesh=mesh,
        in_specs=placed,
        out_specs=(P("section", None, "seq", None), P("seq", None), P("seq", None)),
        check_vma=False,
    )
```
